128 devices in a mesh: row: 8 (over x, z_lo), col: 16 (over z_hi, y, core).
Axes of the slice: x: 4, y: 4, z: 4 (z_hi: 2, z_lo: 2; z = z_hi * 2 + z_lo), core: 2. Of those that a mesh axis runs over, the one named last changes fastest.
Arguments:
- coarse_feat: bfloat16 [1536, 64, 512], P(('row', 'col')), may hold values from -6 to 6
- coarse_children: int32 [1536, 8], P(('row', 'col')), may hold values from -1 to 6143, as said below
- fine_neighbours: int32 [6144, 26], P(('row', 'col')), may hold values from -1 to 6143, as said below
- up_weight: bfloat16 [64, 864], replicated, may hold values from -0.375 to 0.375
- up_bias: float32 [32], replicated, may hold values from -3 to 3
- conv_weight: bfloat16 [32, 864], replicated, may hold values from -0.21875 to 0.21875
- conv_bias: float32 [32], replicated, may hold values from -3 to 3
Outputs:
- fine_features: bfloat16 [6144, 32, 512], P(('row', 'col'))
The draws below stay inside these ranges and needn't reach their ends.
Inputs may be any that keep to these rules, and one draw needn't show every extreme that they name: `coarse_children`: entry [c, o] is the global index of the fine block that is octant o = 4 ox + 2 oy + oz of coarse block c, or -1 when that child is absent. The children present, taken in order of c and then o, are numbered 0, 1, 2 and so on without gaps, so every fine block has exactly one parent and every coarse block has one to seven children. The device holding a fine block is the device holding its parent or one of the two beside it in row-major order of the mesh. `fine_neighbours`: column j stands for direction j of the 26 directions (dx, dy, dz) in the finite set (-1, 0, 1)^3 other than (0, 0, 0) in lexicographic order. The relation is symmetric: if entry [b, j] is n then entry [n, 25 - j] is b. Entries in columns 13 to 25 are larger than b, those in columns 0 to 12 smaller, and every entry lies within 12 of b; so at most 12 blocks of one device have a neighbour on the device after it, and likewise before it.
All inputs are finite; a program needn't handle non-finite values.
Results may differ from the reference program's by a relative error of at most 0.0052.
Values may be sent and summed in bfloat16 or wider, within the bound.
A program may use at most 256 MiB of HBM per device.

```python
import jax
import jax.numpy as jnp
from jax import lax

CIN = 64
COUT = 32
FB_DEV = 48
CB_DEV = 12
KMAX = 12
FBLOCKS = 6144
CBLOCKS = 1536
DEVICES = 128


def draw_coarse_children(key, part):
    key = jax.random.fold_in(key, 11)
    rotation_key, spread_key, order_key = jax.random.split(key, 3)
    groups = DEVICES // 4
    rotation = jax.random.randint(rotation_key, (groups,), 0, 4)
    pattern = jnp.array([6, 5, 3, 2], jnp.int32)
    device_ids = jnp.arange(DEVICES)
    average = pattern[(device_ids % 4 + rotation[device_ids // 4]) % 4]
    spread = jax.random.randint(spread_key, (DEVICES, CB_DEV // 2), -1, 2)
    counts = jnp.stack([average[:, None] + spread, average[:, None] - spread], axis=2).reshape(CBLOCKS)
    scores = jax.random.randint(order_key, (CBLOCKS, 8), 0, 1 << 20) * 8 + jnp.arange(8)
    order_rank = jnp.argsort(jnp.argsort(scores, axis=1), axis=1)
    present = order_rank < counts[:, None]
    within = jnp.cumsum(present.astype(jnp.int32), axis=1) - 1
    starts = jnp.cumsum(counts) - counts
    return jnp.where(present, starts[:, None] + within, -1).astype(jnp.int32)


def draw_fine_neighbours(key, part):
    key = jax.random.fold_in(key, 23)
    stride_key, forced_key, kept_key = jax.random.split(key, 3)
    strides = jax.random.randint(stride_key, (13,), 1, KMAX + 1)
    forced = jax.random.randint(forced_key, (), 0, 13)
    strides = jnp.where(jnp.arange(13) == forced, KMAX, strides)
    retained = jax.random.randint(kept_key, (FBLOCKS, 13), 0, 3) > 0
    block_ids = jnp.arange(FBLOCKS)[:, None]
    upper_ids = block_ids + strides[None, :]
    upper = jnp.where(retained & (upper_ids < FBLOCKS), upper_ids, -1)
    lower_ids = block_ids - strides[None, :]
    lower_kept = retained[jnp.clip(lower_ids, 0, FBLOCKS - 1), jnp.arange(13)[None, :]]
    lower = jnp.where(lower_kept & (lower_ids >= 0), lower_ids, -1)
    return jnp.concatenate([lower[:, ::-1], upper], axis=1).astype(jnp.int32)


def level_of(stream_key, extent, pieces, least, top_value):
    factor_of = 1.0
    for dim, blocks in pieces:
        heights = jax.random.uniform(jax.random.fold_in(jax.random.fold_in(stream_key, 6), dim), (blocks,), jnp.float32, least / len(pieces), top_value / len(pieces))
        factor_of = factor_of * jnp.repeat(jnp.exp(heights), extent[dim] // blocks).reshape((-1,) + (1,) * (len(extent) - 1 - dim))
    return factor_of


def scatter_about(own_key, shape, scale, reach, cuts=(), held_as=jnp.bfloat16):
    entries = scale * jax.random.normal(own_key, shape, jnp.float32)
    if cuts:
        entries = entries * level_of(own_key, shape, cuts, -0.22, 0.18)
    return jnp.clip(entries, -reach, reach).astype(held_as)


def setup_inputs(seed: int = 0) -> dict:
    key_of = jax.random.split(jax.random.key(seed), 8)
    return {
        "coarse_feat": scatter_about(key_of[0], (CBLOCKS, CIN, 512), 1.0, 6.0, ((0, 128),)),
        "coarse_children": draw_coarse_children(jax.random.fold_in(key_of[7], 71), 0),
        "fine_neighbours": draw_fine_neighbours(jax.random.fold_in(key_of[7], 71), 0),
        "up_weight": scatter_about(key_of[3], (CIN, 27 * COUT), (CIN * 4) ** -0.5, 0.375),
        "up_bias": scatter_about(key_of[4], (COUT,), 0.5, 3.0, (), jnp.float32),
        "conv_weight": scatter_about(key_of[5], (COUT, 27 * COUT), (27 * COUT) ** -0.5, 0.21875),
        "conv_bias": scatter_about(key_of[6], (COUT,), 0.5, 3.0, (), jnp.float32),
    }


direction_list = [(code // 9 - 1, code // 3 % 3 - 1, code % 3 - 1) for code in range(27) if code != 13]
upward_list = [(0, 0, 1), (0, 1, 0), (0, 1, 1), (1, 0, 0), (1, 0, 1), (1, 1, 0), (1, 1, 1)]
upward_columns = [9 * (delta[0] + 1) + 3 * (delta[1] + 1) + (delta[2] + 1) - 1 for delta in upward_list]
spill_sizes = [8 ** sum(1 for component in delta if component == 0) for delta in upward_list]
spill_starts = [sum(spill_sizes[:number]) for number in range(7)]


def octant_blocks(coarse_feat):
    count, channels = coarse_feat.shape[0], coarse_feat.shape[1]
    split = coarse_feat.reshape(count, channels, 2, 4, 2, 4, 2, 4)
    moved = jnp.transpose(split, (0, 2, 4, 6, 1, 3, 5, 7))
    return moved.reshape(count * 8, channels * 64)


def place_axis(values, cut_dim):
    inner = cut_dim - 1
    first_tap, middle_tap, last_tap = values[0], values[1], values[2]

    def widen(portion, lower_pad, upper_pad):
        widths = [(0, 0)] * portion.ndim
        widths[inner] = (lower_pad, upper_pad)
        return jnp.pad(portion, widths)

    even_part = widen(first_tap, 0, 1) + widen(last_tap, 1, 0)
    odd_part = widen(middle_tap, 0, 1)
    paired = jnp.stack([even_part, odd_part], axis=inner + 1)
    layout = list(first_tap.shape)
    layout[inner] = 10
    return paired.reshape(layout)


def split_grid(tap_out, cout, count):
    shaped = tap_out.reshape(3, 3, 3, cout, count, 4, 4, 4)
    fine_grid = place_axis(place_axis(place_axis(shaped, 5), 5), 5)
    centre = fine_grid[:, :, 1:9, 1:9, 1:9].reshape(cout, count, 512)
    base = jnp.transpose(centre, (1, 0, 2)).astype(jnp.bfloat16)
    portions = []
    for delta in upward_list:
        picks = tuple(slice(0, 1) if component == 1 else slice(1, 9) for component in delta)
        portions.append(fine_grid[(slice(None), slice(None)) + picks].reshape(cout, count, -1))
    portions.append(jnp.zeros((cout, count, 39), jnp.float32))
    spill = jnp.transpose(jnp.concatenate(portions, axis=2), (1, 0, 2)).astype(jnp.bfloat16)
    return base, spill


def activate(base, beside_spill, up_bias):
    count, cout = base.shape[0], base.shape[1]
    total = base.astype(jnp.float32).reshape(count, cout, 8, 8, 8)
    for number, delta in enumerate(upward_list):
        start = spill_starts[number]
        length = spill_sizes[number]
        layout = (count, cout) + tuple(1 if component == 1 else 8 for component in delta)
        portion = beside_spill[:, number, :, start:start + length].astype(jnp.float32).reshape(layout)
        target = (slice(None), slice(None)) + tuple(slice(7, 8) if component == 1 else slice(0, 8) for component in delta)
        total = total.at[target].add(portion)
    total = total + up_bias[None, :, None, None, None]
    return jax.nn.silu(total).astype(jnp.bfloat16).reshape(count, cout, 512)


def facets(hidden):
    count, cout = hidden.shape[0], hidden.shape[1]
    cube = hidden.reshape(count, cout, 8, 8, 8)
    sheets = [cube[:, :, 0], cube[:, :, 7], cube[:, :, :, 0], cube[:, :, :, 7], cube[:, :, :, :, 0], cube[:, :, :, :, 7]]
    return jnp.concatenate([sheet.reshape(count, cout, 64) for sheet in sheets], axis=2)


def assemble(hidden, beside):
    count, cout = hidden.shape[0], hidden.shape[1]
    cube = hidden.reshape(count, cout, 8, 8, 8)
    padded = jnp.zeros((count, cout, 10, 10, 10), jnp.bfloat16).at[:, :, 1:9, 1:9, 1:9].set(cube)
    for column, delta in enumerate(direction_list):
        which_axis = [number for number in range(3) if delta[number] != 0][0]
        facet_id = 2 * which_axis + (0 if delta[which_axis] == 1 else 1)
        sheet = beside[:, column, :, facet_id * 64:(facet_id + 1) * 64].reshape(count, cout, 8, 8)
        picks = tuple((7 if delta[number] == -1 else (0 if delta[number] == 1 else slice(None))) for number in range(3) if number != which_axis)
        sheet = sheet[(slice(None), slice(None)) + picks]
        target = tuple((0 if component == -1 else (9 if component == 1 else slice(1, 9))) for component in delta)
        padded = padded.at[(slice(None), slice(None)) + target].set(sheet)
    return padded


def gather_patches(padded):
    count, cout = padded.shape[0], padded.shape[1]
    taps = []
    for code in range(27):
        shift_x, shift_y, shift_z = code // 9, code // 3 % 3, code % 3
        taps.append(padded[:, :, shift_x:shift_x + 8, shift_y:shift_y + 8, shift_z:shift_z + 8].reshape(count, cout, 512))
    return jnp.stack(taps, axis=1).reshape(count, 27 * cout, 512)


def reference(coarse_feat, coarse_children, fine_neighbours, up_weight, up_bias, conv_weight, conv_bias):
    total_fine = fine_neighbours.shape[0]
    cin = up_weight.shape[0]
    cout = conv_weight.shape[0]
    octants = octant_blocks(coarse_feat)
    children = coarse_children.reshape(-1)
    source = jnp.zeros((total_fine,), jnp.int32).at[jnp.where(children >= 0, children, total_fine)].set(
        jnp.arange(children.shape[0], dtype=jnp.int32), mode="drop")
    weight_up = up_weight.astype(jnp.float32)

    def upsample_group(sources):
        blocks = octants[sources].reshape(-1, cin, 64).astype(jnp.float32)
        tap_out = jnp.einsum("ck,bcv->kbv", weight_up, blocks, precision=lax.Precision.HIGHEST)
        return split_grid(tap_out, cout, blocks.shape[0])

    base, spill = lax.map(upsample_group, source.reshape(-1, FB_DEV))
    base = base.reshape(total_fine, cout, 512)
    spill = spill.reshape(total_fine, cout, 256)
    spill_table = jnp.concatenate([spill, jnp.zeros((1, cout, 256), jnp.bfloat16)], axis=0)
    all_index = jnp.where(fine_neighbours >= 0, fine_neighbours, total_fine).astype(jnp.int32)
    upward_index = all_index[:, upward_columns]

    def activate_group(inputs):
        base_part, index_part = inputs
        return activate(base_part, spill_table[index_part], up_bias)

    hidden = lax.map(activate_group, (base.reshape(-1, FB_DEV, cout, 512), upward_index.reshape(-1, FB_DEV, 7)))
    hidden = hidden.reshape(total_fine, cout, 512)
    facet_table = jnp.concatenate([facets(hidden), jnp.zeros((1, cout, 384), jnp.bfloat16)], axis=0)
    weight_conv = conv_weight.astype(jnp.float32)

    def conv_group(inputs):
        hidden_part, index_part = inputs
        padded = assemble(hidden_part, facet_table[index_part])
        patches = gather_patches(padded).astype(jnp.float32)
        outputs = jnp.einsum("ok,bkv->obv", weight_conv, patches, precision=lax.Precision.HIGHEST)
        outputs = outputs + conv_bias[:, None, None]
        return jnp.transpose(outputs, (1, 0, 2)).astype(jnp.bfloat16)

    result = lax.map(conv_group, (hidden.reshape(-1, FB_DEV, cout, 512), all_index.reshape(-1, FB_DEV, 26)))
    return result.reshape(total_fine, cout, 512)
```

```python
import jax
import jax.numpy as jnp
from jax import lax
from jax.experimental import pallas as pl
from jax.experimental.pallas import tpu as pltpu
from jax.sharding import PartitionSpec as P

F32 = jnp.float32
BF16 = jnp.bfloat16
AXES = ("row", "col")
HALO = 12
OWN = 48
SLOTS = OWN + 3 * HALO
ACTIVE = OWN + 2 * HALO
REACH = 3 * OWN
EXTRA_AT = 9 * 256
CONV_K = EXTRA_AT + 5 * 128

direction_list = [
    (code // 9 - 1, code // 3 % 3 - 1, code % 3 - 1) for code in range(27) if code != 13
]
column_of = {delta: column for column, delta in enumerate(direction_list)}
upward_list = [(0, 0, 1), (0, 1, 0), (0, 1, 1), (1, 0, 0), (1, 0, 1), (1, 1, 0), (1, 1, 1)]
upward_columns = [column_of[delta] for delta in upward_list]

CLASSES = [
    ((0, 0), 256, 1024 - 256, {(0, 0): (1, 1)}),
    ((0, 1), 256, 1024, {(0, 0): (1, 2), (0, 1): (1, 0)}),
    ((1, 0), 0, 768, {(0, 0): (2, 1), (1, 0): (0, 1)}),
    ((1, 1), 0, 1280, {(0, 0): (2, 2), (0, 1): (2, 0), (1, 0): (0, 2), (1, 1): (0, 0)}),
]
SHIFT_AT = {(1, 0): 0, (0, 0): 512, (0, 1): 768, (1, 1): 1024}
HALO_AT = 256
class_starts = []
UP_K = 0
for _, low, high, _ in CLASSES:
    class_starts.append(UP_K)
    UP_K += high - low


def iota(shape, dim):
    return lax.broadcasted_iota(jnp.int32, shape, dim)


def pack_kernel(place_ref, feat_ref, local_ref, up1_ref, down1_ref, down2_ref, up2_ref, table, source):
    low_lane = iota((64, 128), 1) < 64
    low_row = iota((8, 128), 0) < 4
    table[96] = jnp.zeros((16, 256), BF16)

    def coarse_block(c, _):
        for pair in range(2):
            near = feat_ref[c, :, 128 * pair:128 * pair + 128].astype(F32)
            far = feat_ref[c, :, 256 + 128 * pair:384 + 128 * pair].astype(F32)
            top = jnp.where(low_lane, near, pltpu.roll(far, 64, 1))
            bottom = jnp.where(low_lane, pltpu.roll(near, 64, 1), far)
            turned = jnp.concatenate([top, bottom], axis=0).T
            for octant in range(8):
                ox, oy, oz = octant // 4, octant // 2 % 2, octant % 2
                sheets = []
                for y in range(4):
                    at = 64 * ox + 8 * (4 * oy + y)
                    sheets.append(turned[at:at + 8])
                halves = []
                for one, two in ((sheets[0], sheets[1]), (sheets[2], sheets[3])):
                    if oz == 0:
                        halves.append(jnp.where(low_row, one, pltpu.roll(two, 4, 0)))
                    else:
                        halves.append(jnp.where(low_row, pltpu.roll(one, 4, 0), two))
                table[c * 8 + octant, :, 128 * pair:128 * pair + 128] = jnp.concatenate(
                    halves, axis=0).astype(BF16)
        return 0

    lax.fori_loop(0, feat_ref.shape[0], coarse_block, 0)

    def clear(k, _):
        source[k] = 96
        return 0

    lax.fori_loop(0, REACH + 1, clear, 0, unroll=8)

    def invert(k, _):
        source[place_ref[k]] = k
        return 0

    lax.fori_loop(0, 96, invert, 0, unroll=8)

    for ref, start in ((local_ref, OWN - HALO), (up1_ref, 2 * OWN - HALO), (down1_ref, 0),
                       (down2_ref, 0), (up2_ref, 3 * OWN - HALO)):

        def slot(u, _, ref=ref, start=start):
            ref[u] = table[source[start + u]]
            return 0

        lax.fori_loop(0, ref.shape[0], slot, 0, unroll=4)


def weight_kernel(up_ref, conv_ref, up_out, conv_out):
    spread = (iota((32, 256), 0) == iota((32, 256), 1) % 32).astype(BF16)
    lane_x = iota((32, 256), 1) // 32
    zero = jnp.zeros((32, 256), F32)
    wide = jnp.dot(conv_ref[...], spread, preferred_element_type=F32)

    def tap_of(kx, ky, kz):
        at = 32 * (9 * kx + 3 * ky + kz)
        return wide[at:at + 32]

    for ky in range(3):
        for kz in range(3):
            taps = [tap_of(kx, ky, kz) for kx in range(3)]
            for x in range(8):
                value = zero
                for kx in range(3):
                    value = jnp.where(lane_x == x + 1 - kx, taps[kx], value)
                at = 256 * (3 * ky + kz) + 32 * x
                conv_out[at:at + 32] = value.astype(BF16)
    pairs = [((0, 0), (0, 1)), ((1, 0), (1, 1)), ((2, 0), (2, 1)), ((0, 2), (1, 2)), ((2, 2), None)]
    for tile, (even, odd) in enumerate(pairs):
        at = EXTRA_AT + 128 * tile

        def beyond(tap):
            return zero if tap is None else jnp.where(lane_x == 7, tap_of(2, *tap), zero)

        def before(tap):
            return zero if tap is None else jnp.where(lane_x == 0, tap_of(0, *tap), zero)

        conv_out[at:at + 32] = beyond(even).astype(BF16)
        conv_out[at + 32:at + 64] = before(odd).astype(BF16)
        conv_out[at + 64:at + 96] = beyond(odd).astype(BF16)
        conv_out[at + 96:at + 128] = before(even).astype(BF16)

    lane_f = iota((64, 256), 1) // 32
    zero_up = jnp.zeros((64, 256), F32)

    def up_tap(kx, ky, kz):
        code = 9 * kx + 3 * ky + kz
        return jnp.dot(up_ref[:, 32 * code:32 * code + 32], spread, preferred_element_type=F32)

    for (_, low, high, taps_of), start in zip(CLASSES, class_starts):
        for shift, at_lane in SHIFT_AT.items():
            if not low <= at_lane < high:
                continue
            at = start + at_lane - low
            taps = [up_tap(kx, *taps_of[shift]) for kx in range(3)]
            for x in range(4):
                value = zero_up
                for kx in range(3):
                    value = jnp.where(lane_f == 2 * x + kx - 1, taps[kx], value)
                up_out[at + 64 * x:at + 64 * x + 64] = value.astype(BF16)
        for number, shift in enumerate(((0, 0), (0, 1), (1, 0), (1, 1))):
            at = start + HALO_AT - low + 64 * number
            value = zero_up
            if shift in taps_of:
                value = jnp.where(lane_f == 7, up_tap(0, *taps_of[shift]), zero_up)
            up_out[at:at + 64] = value.astype(BF16)


def main_kernel(near7_ref, near26_ref, local_ref, up1_ref, down1_ref, down2_ref, up2_ref, up_w, up_b,
                conv_w, conv_b, out_ref, octs, shifted, hidden, patches):
    octs[SLOTS] = jnp.zeros((16, 256), F32)

    def join(parts):
        def body(u, _):
            total = local_ref[u].astype(F32)
            for ref, offset in parts:
                total = total + ref[u - offset].astype(F32)
            octs[u] = total
            return 0
        return body

    lax.fori_loop(0, HALO, join([(up1_ref, 0), (up2_ref, 0)]), 0, unroll=2)
    lax.fori_loop(HALO, OWN + HALO, join([(up1_ref, 0), (down1_ref, HALO)]), 0, unroll=4)
    lax.fori_loop(OWN + HALO, SLOTS, join([(down1_ref, HALO), (down2_ref, OWN + HALO)]), 0, unroll=2)

    def shift_z(value, beyond):
        last = iota(value.shape, 0) % 4 == 3
        return jnp.where(last, pltpu.roll(beyond, 3, 0), pltpu.roll(value, 15, 0))

    def shift_y(value, beyond):
        first = iota(value.shape, 0) < 4
        return pltpu.roll(jnp.where(first, beyond, value), 12, 0)

    low_lane16 = iota((16, 128), 1) < 64

    def spread_octant(h, _):
        at = [near7_ref[h * 7 + j] for j in range(7)]
        here, z_next, y_next, yz_next = octs[h], octs[at[0]], octs[at[1]], octs[at[2]]
        by_z = shift_z(here, z_next)
        shifted[h, :, 512:768] = here.astype(BF16)
        shifted[h, :, 768:1024] = by_z.astype(BF16)
        shifted[h, :, 0:256] = shift_y(here, y_next).astype(BF16)
        shifted[h, :, 1024:1280] = shift_y(by_z, shift_z(y_next, yz_next)).astype(BF16)
        x0, xz, xy, xyz = [octs[at[j], :, 0:128] for j in (3, 4, 5, 6)]
        x_by_z = shift_z(x0, xz)
        x_by_y = shift_y(x0, xy)
        x_by_yz = shift_y(x_by_z, shift_z(xy, xyz))
        shifted[h, :, 256:384] = jnp.where(low_lane16, x0, pltpu.roll(x_by_z, 64, 1)).astype(BF16)
        shifted[h, :, 384:512] = jnp.where(low_lane16, x_by_y, pltpu.roll(x_by_yz, 64, 1)).astype(BF16)
        return 0

    lax.fori_loop(0, ACTIVE, spread_octant, 0)

    hidden[:, ACTIVE] = jnp.zeros((2, 64, 128), F32)
    up_bias = up_b[...]

    def upsample(chunk, _):
        for ((py, pz), low, high, _), start in zip(CLASSES, class_starts):
            rows = shifted[pl.ds(chunk * 8, 8), :, low:high].reshape(128, high - low)
            value = jnp.dot(rows, up_w[start:start + high - low], preferred_element_type=F32) + up_bias
            half = 0.5 * value
            value = half + half * jnp.tanh(half)
            for b in range(8):
                for y in range(4):
                    part = value[16 * b + 4 * y:16 * b + 4 * y + 4]
                    for tile in range(2):
                        hidden[tile, chunk * 8 + b, pl.ds(8 * (2 * y + py) + pz, 4, stride=2), :] = (
                            part[:, 128 * tile:128 * tile + 128])
        return 0

    lax.fori_loop(0, ACTIVE // 8, upsample, 0)

    conv_bias = conv_b[...]
    row = iota((8, 128), 0)
    first_row, last_row = row == 0, row == 7
    low_lane8 = iota((8, 128), 1) < 64
    lane = iota((8, 128), 1)
    even_lane = (lane < 32) | (lane >= 96)
    low_lane32 = iota((32, 128), 1) < 64

    def shift_row(dz, value, beyond):
        if dz == 0:
            return value
        if dz == 1:
            return pltpu.roll(jnp.where(first_row, beyond, value), 7, 0)
        return pltpu.roll(jnp.where(last_row, beyond, value), 1, 0)

    def two(one, other):
        return jnp.concatenate([one, other], axis=0).astype(BF16)

    def build(base, b, k):
        at = {delta: near26_ref[b * 26 + column] for delta, column in column_of.items()}
        at[(0, 0, 0)] = b + HALO

        def sheet(delta, y, tile):
            return hidden[tile, at[delta], 8 * y:8 * y + 8, :]

        def side(dy, dz, y):
            return jnp.where(low_lane8, sheet((1, dy, dz), y, 0), sheet((-1, dy, dz), y, 1))

        def sheets(dz, take):
            listed = []
            for step in range(10):
                dy = -1 if step == 0 else (1 if step == 9 else 0)
                y = (step - 1) % 8
                beyond = None if dz == 0 else take(dy, dz, y)
                listed.append(shift_row(dz, take(dy, 0, y), beyond))
            return listed

        def put(values, ky, at_lane):
            for pair in range(4):
                patches[k, 16 * pair:16 * pair + 16, at_lane:at_lane + 128] = values[pair]

        def put_all(listed, lanes):
            even = [two(listed[2 * n], listed[2 * n + 1]) for n in range(5)]
            odd = [two(listed[2 * n + 1], listed[2 * n + 2]) for n in range(4)]
            put(even[0:4], 0, lanes[0])
            put(odd, 1, lanes[1])
            put(even[1:5], 2, lanes[2])

        for dz in (-1, 0, 1):
            for tile in range(2):
                listed = sheets(dz, lambda dy, dz_, y: sheet((0, dy, dz_), y, tile))
                put_all(listed, [256 * (3 * ky + dz + 1) + 128 * tile for ky in range(3)])
        sides = [sheets(dz, side) for dz in (-1, 0, 1)]
        joined = [jnp.where(even_lane, one, pltpu.roll(other, 64, 1)) for one, other in zip(sides[0], sides[1])]
        put_all(joined, [EXTRA_AT + 128 * ky for ky in range(3)])
        last = sides[2]
        paired = [jnp.where(even_lane, last[n], pltpu.roll(last[n + 1], 64, 1)) for n in range(8)]
        put([two(paired[2 * n], paired[2 * n + 1]) for n in range(4)], 0, EXTRA_AT + 384)
        put([two(last[2 * n + 2], last[2 * n + 3]) for n in range(4)], 0, EXTRA_AT + 512)

    def convolve(chunk, _):
        base = chunk * 4
        for k in range(4):
            build(base, base + k, k)
        value = jnp.dot(patches[...].reshape(256, CONV_K), conv_w[...], preferred_element_type=F32) + conv_bias
        for pair in range(2):
            for half in range(2):
                turned = value[128 * pair:128 * pair + 128, 128 * half:128 * half + 128].T
                for x in range(0, 4, 2):
                    one, other = turned[32 * x:32 * x + 32], turned[32 * x + 32:32 * x + 64]
                    at = 256 * half + 64 * x
                    b = base + 2 * pair
                    out_ref[b, :, at:at + 128] = jnp.where(
                        low_lane32, one, pltpu.roll(other, 64, 1)).astype(BF16)
                    out_ref[b + 1, :, at:at + 128] = jnp.where(
                        low_lane32, pltpu.roll(one, 64, 1), other).astype(BF16)
        return 0

    lax.fori_loop(0, OWN // 4, convolve, 0)


def passed_along(block, distance):
    devices = range(lax.axis_size(AXES))
    route = [(i - distance, i) for i in devices if i - distance in devices]
    return lax.ppermute(block, AXES, route)


VMEM = pl.BlockSpec(memory_space=pltpu.VMEM)
SMEM = pl.BlockSpec(memory_space=pltpu.SMEM)


def on_device(
    coarse_feat, coarse_children, fine_neighbours, up_weight, up_bias, conv_weight, conv_bias
):
    rank = lax.axis_index(AXES)
    children = coarse_children.reshape(-1)
    place = jnp.where(children >= 0, children - (rank - 1) * OWN, REACH)
    own_ids = rank * OWN + lax.broadcasted_iota(jnp.int32, (OWN, 1), 0)
    upward = fine_neighbours[:, jnp.array(upward_columns)]
    upward = jnp.where(upward >= 0, upward - own_ids, 0)
    before = passed_along(upward[OWN - HALO:], 1)
    after = passed_along(upward[:HALO], -1)
    upward = jnp.concatenate([before, upward, after], axis=0)
    near7 = jnp.where(upward > 0, upward + lax.broadcasted_iota(jnp.int32, (ACTIVE, 1), 0), SLOTS)
    near26 = jnp.where(fine_neighbours >= 0, fine_neighbours - (rank * OWN - HALO), ACTIVE)

    counts = (SLOTS, OWN + HALO, OWN + 2 * HALO, 2 * HALO, HALO)
    local, up1, down1, down2, up2 = pl.pallas_call(
        pack_kernel,
        out_shape=[jax.ShapeDtypeStruct((count, 16, 256), BF16) for count in counts],
        in_specs=[SMEM, VMEM],
        out_specs=[VMEM] * 5,
        scratch_shapes=[pltpu.VMEM((97, 16, 256), BF16), pltpu.SMEM((REACH + 8,), jnp.int32)],
        compiler_params=pltpu.CompilerParams(vmem_limit_bytes=24 * 2 ** 20),
        name="pack",
    )(place, coarse_feat)
    up1 = passed_along(up1, 1)
    down1 = passed_along(down1, -1)
    down2 = passed_along(down2, -2)
    up2 = passed_along(up2, 2)

    up_w, conv_w = pl.pallas_call(
        weight_kernel,
        out_shape=[jax.ShapeDtypeStruct((UP_K, 256), BF16), jax.ShapeDtypeStruct((CONV_K, 256), BF16)],
        in_specs=[VMEM, VMEM],
        out_specs=[VMEM, VMEM],
        compiler_params=pltpu.CompilerParams(vmem_limit_bytes=24 * 2 ** 20),
        cost_estimate=pl.CostEstimate(flops=10 ** 9, bytes_accessed=4 * 10 ** 6, transcendentals=0),
        name="weights",
    )(up_weight, conv_weight.T)

    return pl.pallas_call(
        main_kernel,
        out_shape=jax.ShapeDtypeStruct((OWN, 32, 512), BF16),
        in_specs=[SMEM, SMEM] + [VMEM] * 9,
        out_specs=VMEM,
        scratch_shapes=[
            pltpu.VMEM((SLOTS + 1, 16, 256), F32),
            pltpu.VMEM((ACTIVE, 16, 1280), BF16),
            pltpu.VMEM((2, ACTIVE + 1, 64, 128), F32),
            pltpu.VMEM((4, 64, CONV_K), BF16),
        ],
        compiler_params=pltpu.CompilerParams(vmem_limit_bytes=48 * 2 ** 20),
        name="convolutions",
    )(near7.reshape(-1), near26.reshape(-1), local, up1, down1, down2, up2,
      up_w, jnp.tile(up_bias, 8)[None, :], conv_w, jnp.tile(conv_bias, 8)[None, :])


def solution(mesh):
    in_specs = (
        P(AXES, None, None),
        P(AXES, None),
        P(AXES, None),
        P(),
        P(),
        P(),
        P(),
    )
    return jax.shard_map(
        on_device, mesh=mesh, in_specs=in_specs, out_specs=P(AXES, None, None), check_vma=False
    )
```

```python
import jax
import jax.numpy as jnp
from jax import lax
from jax.experimental import pallas as pl
from jax.experimental.pallas import tpu as pltpu
from jax.sharding import PartitionSpec as P

F32 = jnp.float32
BF16 = jnp.bfloat16
AXES = ("row", "col")
HALO = 12
OWN = 48
SLOTS = OWN + 3 * HALO
ACTIVE = OWN + 2 * HALO
REACH = 3 * OWN
SPREAD = 4
UP = 24
GROUP = 4
EXTRA_AT = 9 * 256
CONV_K = EXTRA_AT + 5 * 128

direction_list = [
    (code // 9 - 1, code // 3 % 3 - 1, code % 3 - 1) for code in range(27) if code != 13
]
column_of = {delta: column for column, delta in enumerate(direction_list)}
upward_list = [(0, 0, 1), (0, 1, 0), (0, 1, 1), (1, 0, 0), (1, 0, 1), (1, 1, 0), (1, 1, 1)]
upward_columns = [column_of[delta] for delta in upward_list]

CLASSES = [
    ((0, 0), 256, 1024 - 256, {(0, 0): (1, 1)}),
    ((0, 1), 256, 1024, {(0, 0): (1, 2), (0, 1): (1, 0)}),
    ((1, 0), 0, 768, {(0, 0): (2, 1), (1, 0): (0, 1)}),
    ((1, 1), 0, 1280, {(0, 0): (2, 2), (0, 1): (2, 0), (1, 0): (0, 2), (1, 1): (0, 0)}),
]
SHIFT_AT = {(1, 0): 0, (0, 0): 512, (0, 1): 768, (1, 1): 1024}
HALO_AT = 256
class_starts = []
UP_K = 0
for _, low, high, _ in CLASSES:
    class_starts.append(UP_K)
    UP_K += high - low


def iota(shape, dim):
    return lax.broadcasted_iota(jnp.int32, shape, dim)


def exchange_kernel(children_ref, near_ref, feat_ref, up_ref, conv_ref, octs_ref, near_out, up_hbm, conv_hbm,
                    table, slots, source_v, source, from1, from_1, from_2, from2, near_prev, near_next,
                    up_out, conv_out, send_sem, recv_sem, local_sem, weight_sem):
    ranks = lax.axis_size("row") * lax.axis_size("col")
    rank = lax.axis_index("row") * lax.axis_size("col") + lax.axis_index("col")

    def device(offset):
        other = lax.rem(rank + offset + ranks, ranks)
        return other // lax.axis_size("col"), lax.rem(other, lax.axis_size("col"))

    barrier = pltpu.get_barrier_semaphore()
    for offset in (1, -1, 2, -2):
        pl.semaphore_signal(barrier, inc=1, device_id=device(offset), device_id_type=pl.DeviceIdType.MESH)

    slot_id = iota((8, 128), 0) * 128 + iota((8, 128), 1)
    first = (rank - 1) * OWN
    chosen = jnp.full((8, 128), 96, jnp.int32)
    for c in range(12):
        for o in range(8):
            child = children_ref[c, o]
            position = jnp.where(child >= 0, child - first, REACH)
            chosen = jnp.where(slot_id == position, 8 * c + o, chosen)
    source_v[...] = chosen
    fetch = pltpu.make_async_copy(source_v, source, local_sem)
    fetch.start()

    low_lane = iota((64, 128), 1) < 64
    low_row = iota((8, 128), 0) < 4
    table[96] = jnp.zeros((16, 256), BF16)

    def coarse_block(c, _):
        for pair in range(2):
            near = feat_ref[c, :, 128 * pair:128 * pair + 128].astype(F32)
            far = feat_ref[c, :, 256 + 128 * pair:384 + 128 * pair].astype(F32)
            top = jnp.where(low_lane, near, pltpu.roll(far, 64, 1))
            bottom = jnp.where(low_lane, pltpu.roll(near, 64, 1), far)
            turned = jnp.concatenate([top, bottom], axis=0).T
            for octant in range(8):
                ox, oy, oz = octant // 4, octant // 2 % 2, octant % 2
                sheets = []
                for y in range(4):
                    at = 64 * ox + 8 * (4 * oy + y)
                    sheets.append(turned[at:at + 8])
                halves = []
                for one, two in ((sheets[0], sheets[1]), (sheets[2], sheets[3])):
                    if oz == 0:
                        halves.append(jnp.where(low_row, one, pltpu.roll(two, 4, 0)))
                    else:
                        halves.append(jnp.where(low_row, pltpu.roll(one, 4, 0), two))
                table[c * 8 + octant, :, 128 * pair:128 * pair + 128] = jnp.concatenate(
                    halves, axis=0).astype(BF16)
        return 0

    lax.fori_loop(0, feat_ref.shape[0], coarse_block, 0)

    fetch.wait()

    def fill(k, _):
        for j in range(4):
            q = k * 4 + j
            slots[q] = table[source[q // 128, q % 128]]
        return 0

    lax.fori_loop(0, REACH // 4, fill, 0)

    pl.semaphore_wait(barrier, 4)
    copies = []
    for number, (src, dst, offset) in enumerate((
            (slots.at[0:OWN + 2 * HALO], from_1, -1),
            (slots.at[2 * OWN - HALO:REACH], from1, 1),
            (slots.at[0:2 * HALO], from_2, -2),
            (slots.at[REACH - HALO:REACH], from2, 2),
            (near_ref.at[0:16], near_next, -1),
            (near_ref.at[OWN - 16:OWN], near_prev, 1))):
        copy = pltpu.make_async_remote_copy(
            src_ref=src, dst_ref=dst, send_sem=send_sem.at[number], recv_sem=recv_sem.at[number],
            device_id=device(offset), device_id_type=pl.DeviceIdType.MESH)
        copy.start()
        copies.append(copy)

    make_weights(up_ref, conv_ref, up_out, conv_out)
    up_copy = pltpu.make_async_copy(up_out, up_hbm, weight_sem.at[0])
    conv_copy = pltpu.make_async_copy(conv_out, conv_hbm, weight_sem.at[1])
    up_copy.start()
    conv_copy.start()

    def relative(value):
        moved = value - (rank * OWN - HALO)
        return jnp.where((value >= 0) & (moved >= 0) & (moved < SLOTS), moved, SLOTS)

    near_out[16:16 + OWN] = relative(near_ref[...])
    octs_ref[SLOTS] = jnp.zeros((16, 256), F32)
    for copy in copies[4:] + copies[:4]:
        copy.wait()
    near_out[0:16] = relative(near_prev[...])
    near_out[16 + OWN:32 + OWN] = relative(near_next[...])

    def join(parts):
        def body(u, _):
            total = slots[u + OWN - HALO].astype(F32)
            for ref, offset in parts:
                total = total + ref[u - offset].astype(F32)
            octs_ref[u] = total
            return 0
        return body

    lax.fori_loop(0, HALO, join([(from1, 0), (from2, 0)]), 0, unroll=4)
    lax.fori_loop(HALO, OWN + HALO, join([(from1, 0), (from_1, HALO)]), 0, unroll=8)
    lax.fori_loop(OWN + HALO, SLOTS, join([(from_1, HALO), (from_2, OWN + HALO)]), 0, unroll=4)
    up_copy.wait()
    conv_copy.wait()


def make_weights(up_ref, conv_ref, up_out, conv_out):
    spread = (iota((32, 256), 0) == iota((32, 256), 1) % 32).astype(BF16)
    lane_x = iota((32, 256), 1) // 32
    zero = jnp.zeros((32, 256), F32)
    wide = lax.dot_general(conv_ref[...], spread, (((0,), (0,)), ((), ())), preferred_element_type=F32)

    def tap_of(kx, ky, kz):
        at = 32 * (9 * kx + 3 * ky + kz)
        return wide[at:at + 32]

    for ky in range(3):
        for kz in range(3):
            taps = [tap_of(kx, ky, kz) for kx in range(3)]
            for x in range(8):
                value = zero
                for kx in range(3):
                    value = jnp.where(lane_x == x + 1 - kx, taps[kx], value)
                at = 256 * (3 * ky + kz) + 32 * x
                conv_out[at:at + 32] = value.astype(BF16)
    pairs = [((0, 0), (0, 1)), ((1, 0), (1, 1)), ((2, 0), (2, 1)), ((0, 2), (1, 2)), ((2, 2), None)]
    for tile, (even, odd) in enumerate(pairs):
        at = EXTRA_AT + 128 * tile

        def beyond(tap):
            return zero if tap is None else jnp.where(lane_x == 7, tap_of(2, *tap), zero)

        def before(tap):
            return zero if tap is None else jnp.where(lane_x == 0, tap_of(0, *tap), zero)

        conv_out[at:at + 32] = beyond(even).astype(BF16)
        conv_out[at + 32:at + 64] = before(odd).astype(BF16)
        conv_out[at + 64:at + 96] = beyond(odd).astype(BF16)
        conv_out[at + 96:at + 128] = before(even).astype(BF16)

    lane_f = iota((64, 256), 1) // 32
    zero_up = jnp.zeros((64, 256), F32)

    def up_tap(kx, ky, kz):
        code = 9 * kx + 3 * ky + kz
        return jnp.dot(up_ref[:, 32 * code:32 * code + 32], spread, preferred_element_type=F32)

    for (_, low, high, taps_of), start in zip(CLASSES, class_starts):
        for shift, at_lane in SHIFT_AT.items():
            if not low <= at_lane < high:
                continue
            at = start + at_lane - low
            taps = [up_tap(kx, *taps_of[shift]) for kx in range(3)]
            for x in range(4):
                value = zero_up
                for kx in range(3):
                    value = jnp.where(lane_f == 2 * x + kx - 1, taps[kx], value)
                up_out[at + 64 * x:at + 64 * x + 64] = value.astype(BF16)
        for number, shift in enumerate(((0, 0), (0, 1), (1, 0), (1, 1))):
            at = start + HALO_AT - low + 64 * number
            value = zero_up
            if shift in taps_of:
                value = jnp.where(lane_f == 7, up_tap(0, *taps_of[shift]), zero_up)
            up_out[at:at + 64] = value.astype(BF16)


def main_kernel(near_ref, octs, up_hbm, up_b, conv_hbm, conv_b, out_ref, up_w, conv_w, shifted, hidden,
                patches_0, patches_1, weight_sem):
    up_copy = pltpu.make_async_copy(up_hbm, up_w, weight_sem.at[0])
    conv_copy = pltpu.make_async_copy(conv_hbm, conv_w, weight_sem.at[1])
    up_copy.start()
    conv_copy.start()
    spread = (iota((32, 256), 0) == iota((32, 256), 1) % 32).astype(F32)

    def wide_bias(ref):
        return jnp.dot(jnp.broadcast_to(ref[...], (8, 32)), spread, precision=lax.Precision.HIGHEST,
                       preferred_element_type=F32)[0:1]

    def shift_z(value, beyond):
        last = iota(value.shape, 0) % 4 == 3
        return jnp.where(last, pltpu.roll(beyond, 3, 0), pltpu.roll(value, 15, 0))

    def shift_y(value, beyond):
        first = iota(value.shape, 0) < 4
        return pltpu.roll(jnp.where(first, beyond, value), 12, 0)

    low_lane16 = iota((16, 128), 1) < 64

    def spread_octant(h):
        at = [near_ref[h + 4, column] for column in upward_columns]
        here, z_next, y_next, yz_next = octs[h], octs[at[0]], octs[at[1]], octs[at[2]]
        by_z = shift_z(here, z_next)
        x0, xz, xy, xyz = [octs[at[j], :, 0:128] for j in (3, 4, 5, 6)]
        x_by_z = shift_z(x0, xz)
        x_by_y = shift_y(x0, xy)
        x_by_yz = shift_y(x_by_z, shift_z(xy, xyz))
        return [
            (0, shift_y(here, y_next)),
            (256, jnp.where(low_lane16, x0, pltpu.roll(x_by_z, 64, 1))),
            (384, jnp.where(low_lane16, x_by_y, pltpu.roll(x_by_yz, 64, 1))),
            (512, here),
            (768, by_z),
            (1024, shift_y(by_z, shift_z(y_next, yz_next))),
        ]

    def spread_octants(group, _):
        for h, parts in [(group * SPREAD + k, spread_octant(group * SPREAD + k)) for k in range(SPREAD)]:
            for lane, value in parts:
                shifted[h, :, lane:lane + value.shape[1]] = value.astype(BF16)
        return 0

    lax.fori_loop(0, ACTIVE // SPREAD, spread_octants, 0)
    up_copy.wait()

    hidden[:, SLOTS] = jnp.zeros((2, 64, 128), F32)
    up_bias = wide_bias(up_b)

    def upsample(chunk, _):
        for ((py, pz), low, high, _), start in zip(CLASSES, class_starts):
            rows = shifted[pl.ds(chunk * UP, UP), :, low:high].reshape(16 * UP, high - low)
            value = jnp.dot(rows, up_w[start:start + high - low], preferred_element_type=F32) + up_bias
            half = 0.5 * value
            value = half + half * jnp.tanh(half)
            for b in range(UP):
                for y in range(4):
                    part = value[16 * b + 4 * y:16 * b + 4 * y + 4]
                    for tile in range(2):
                        hidden[tile, chunk * UP + b, pl.ds(8 * (2 * y + py) + pz, 4, stride=2), :] = (
                            part[:, 128 * tile:128 * tile + 128])
        return 0

    lax.fori_loop(0, ACTIVE // UP, upsample, 0)
    conv_copy.wait()

    conv_bias = wide_bias(conv_b)
    row = iota((8, 128), 0)
    first_row, last_row = row == 0, row == 7
    low_lane8 = iota((8, 128), 1) < 64
    lane = iota((8, 128), 1)
    even_lane = (lane < 32) | (lane >= 96)
    low_lane32 = iota((32, 128), 1) < 64

    def shift_row(dz, value, beyond):
        if dz == 0:
            return value
        if dz == 1:
            return pltpu.roll(jnp.where(first_row, beyond, value), 7, 0)
        return pltpu.roll(jnp.where(last_row, beyond, value), 1, 0)

    def two(one, other):
        return jnp.concatenate([one, other], axis=0).astype(BF16)

    def build(patches, b, k):
        at = {delta: near_ref[b + 16, column] for delta, column in column_of.items()}
        at[(0, 0, 0)] = b + HALO

        def sheet(delta, y, tile):
            return hidden[tile, at[delta], 8 * y:8 * y + 8, :]

        def side(dy, dz, y):
            return jnp.where(low_lane8, sheet((1, dy, dz), y, 0), sheet((-1, dy, dz), y, 1))

        def sheets(dz, take):
            listed = []
            for step in range(10):
                dy = -1 if step == 0 else (1 if step == 9 else 0)
                y = (step - 1) % 8
                beyond = None if dz == 0 else take(dy, dz, y)
                listed.append(shift_row(dz, take(dy, 0, y), beyond))
            return listed

        def put(values, ky, at_lane):
            for pair in range(4):
                patches[k, 16 * pair:16 * pair + 16, at_lane:at_lane + 128] = values[pair]

        def put_all(listed, lanes):
            even = [two(listed[2 * n], listed[2 * n + 1]) for n in range(5)]
            odd = [two(listed[2 * n + 1], listed[2 * n + 2]) for n in range(4)]
            put(even[0:4], 0, lanes[0])
            put(odd, 1, lanes[1])
            put(even[1:5], 2, lanes[2])

        for dz in (-1, 0, 1):
            for tile in range(2):
                listed = sheets(dz, lambda dy, dz_, y: sheet((0, dy, dz_), y, tile))
                put_all(listed, [256 * (3 * ky + dz + 1) + 128 * tile for ky in range(3)])
        sides = [sheets(dz, side) for dz in (-1, 0, 1)]
        joined = [jnp.where(even_lane, one, pltpu.roll(other, 64, 1)) for one, other in zip(sides[0], sides[1])]
        put_all(joined, [EXTRA_AT + 128 * ky for ky in range(3)])
        last = sides[2]
        paired = [jnp.where(even_lane, last[n], pltpu.roll(last[n + 1], 64, 1)) for n in range(8)]
        put([two(paired[2 * n], paired[2 * n + 1]) for n in range(4)], 0, EXTRA_AT + 384)
        put([two(last[2 * n + 2], last[2 * n + 3]) for n in range(4)], 0, EXTRA_AT + 512)

    def convolve(patches, base):
        value = jnp.dot(patches[...].reshape(64 * GROUP, CONV_K), conv_w[...], preferred_element_type=F32) + conv_bias
        for pair in range(GROUP // 2):
            for half in range(2):
                turned = value[128 * pair:128 * pair + 128, 128 * half:128 * half + 128].T
                for x in range(0, 4, 2):
                    one, other = turned[32 * x:32 * x + 32], turned[32 * x + 32:32 * x + 64]
                    at = 256 * half + 64 * x
                    b = base + 2 * pair
                    out_ref[b, :, at:at + 128] = jnp.where(
                        low_lane32, one, pltpu.roll(other, 64, 1)).astype(BF16)
                    out_ref[b + 1, :, at:at + 128] = jnp.where(
                        low_lane32, pltpu.roll(one, 64, 1), other).astype(BF16)

    def build_group(patches, base):
        for k in range(GROUP):
            build(patches, base + k, k)

    build_group(patches_0, 0)

    def groups(step, _):
        base = step * 2 * GROUP
        build_group(patches_1, base + GROUP)
        convolve(patches_0, base)
        build_group(patches_0, jnp.minimum(base + 2 * GROUP, OWN - GROUP))
        convolve(patches_1, base + GROUP)
        return 0

    lax.fori_loop(0, OWN // (2 * GROUP), groups, 0)


VMEM = pl.BlockSpec(memory_space=pltpu.VMEM)
SMEM = pl.BlockSpec(memory_space=pltpu.SMEM)
ANY = pl.BlockSpec(memory_space=pl.ANY)


def on_device(
    coarse_feat, coarse_children, fine_neighbours, up_weight, up_bias, conv_weight, conv_bias
):
    octs, near, up_w, conv_w = pl.pallas_call(
        exchange_kernel,
        out_shape=[
            jax.ShapeDtypeStruct((SLOTS + 1, 16, 256), F32),
            jax.ShapeDtypeStruct((OWN + 32, 26), jnp.int32),
            jax.ShapeDtypeStruct((UP_K, 256), BF16),
            jax.ShapeDtypeStruct((CONV_K, 256), BF16),
        ],
        in_specs=[SMEM, VMEM, VMEM, VMEM, VMEM],
        out_specs=[VMEM, VMEM, ANY, ANY],
        scratch_shapes=[
            pltpu.VMEM((97, 16, 256), BF16),
            pltpu.VMEM((REACH, 16, 256), BF16),
            pltpu.VMEM((8, 128), jnp.int32),
            pltpu.SMEM((8, 128), jnp.int32),
            pltpu.VMEM((OWN + HALO, 16, 256), BF16),
            pltpu.VMEM((OWN + 2 * HALO, 16, 256), BF16),
            pltpu.VMEM((2 * HALO, 16, 256), BF16),
            pltpu.VMEM((HALO, 16, 256), BF16),
            pltpu.VMEM((16, 26), jnp.int32),
            pltpu.VMEM((16, 26), jnp.int32),
            pltpu.VMEM((UP_K, 256), BF16),
            pltpu.VMEM((CONV_K, 256), BF16),
            pltpu.SemaphoreType.DMA((6,)),
            pltpu.SemaphoreType.DMA((6,)),
            pltpu.SemaphoreType.DMA,
            pltpu.SemaphoreType.DMA((2,)),
        ],
        compiler_params=pltpu.CompilerParams(
            vmem_limit_bytes=40 * 2 ** 20, collective_id=0, has_side_effects=True),
        name="exchange",
    )(coarse_children, fine_neighbours, coarse_feat, up_weight, conv_weight)
    return pl.pallas_call(
        main_kernel,
        out_shape=jax.ShapeDtypeStruct((OWN, 32, 512), BF16),
        in_specs=[SMEM, VMEM, ANY, VMEM, ANY, VMEM],
        out_specs=VMEM,
        scratch_shapes=[
            pltpu.VMEM((UP_K, 256), BF16),
            pltpu.VMEM((CONV_K, 256), BF16),
            pltpu.VMEM((ACTIVE, 16, 1280), BF16),
            pltpu.VMEM((2, SLOTS + 1, 64, 128), F32),
            pltpu.VMEM((GROUP, 64, CONV_K), BF16),
            pltpu.VMEM((GROUP, 64, CONV_K), BF16),
            pltpu.SemaphoreType.DMA((2,)),
        ],
        compiler_params=pltpu.CompilerParams(vmem_limit_bytes=48 * 2 ** 20),
        name="convolutions",
    )(near, octs, up_w, up_bias[None, :], conv_w, conv_bias[None, :])


def solution(mesh):
    in_specs = (
        P(AXES, None, None),
        P(AXES, None),
        P(AXES, None),
        P(),
        P(),
        P(),
        P(),
    )
    return jax.shard_map(
        on_device, mesh=mesh, in_specs=in_specs, out_specs=P(AXES, None, None), check_vma=False
    )
```

```python
import jax
import jax.numpy as jnp
from jax import lax
from jax.experimental import pallas as pl
from jax.experimental.pallas import tpu as pltpu
from jax.sharding import PartitionSpec as P

F32 = jnp.float32
BF16 = jnp.bfloat16
AXES = ("row", "col")
HALO = 12
OWN = 48
SLOTS = OWN + 3 * HALO
ACTIVE = OWN + 2 * HALO
REACH = 3 * OWN
PACK = 3
SPREAD = 6
UP = 24
GROUP = 8
EXTRA_AT = 9 * 256
CONV_K = EXTRA_AT + 5 * 128

direction_list = [
    (code // 9 - 1, code // 3 % 3 - 1, code % 3 - 1) for code in range(27) if code != 13
]
column_of = {delta: column for column, delta in enumerate(direction_list)}
upward_list = [(0, 0, 1), (0, 1, 0), (0, 1, 1), (1, 0, 0), (1, 0, 1), (1, 1, 0), (1, 1, 1)]
upward_columns = [column_of[delta] for delta in upward_list]

CLASSES = [
    ((0, 0), 256, 1024 - 256, {(0, 0): (1, 1)}),
    ((0, 1), 256, 1024, {(0, 0): (1, 2), (0, 1): (1, 0)}),
    ((1, 0), 0, 768, {(0, 0): (2, 1), (1, 0): (0, 1)}),
    ((1, 1), 0, 1280, {(0, 0): (2, 2), (0, 1): (2, 0), (1, 0): (0, 2), (1, 1): (0, 0)}),
]
SHIFT_AT = {(1, 0): 0, (0, 0): 512, (0, 1): 768, (1, 1): 1024}
HALO_AT = 256
class_starts = []
UP_K = 0
for _, low, high, _ in CLASSES:
    class_starts.append(UP_K)
    UP_K += high - low


def iota(shape, dim):
    return lax.broadcasted_iota(jnp.int32, shape, dim)


def exchange_kernel(children_hbm, near_hbm, feat_hbm, up_hbm, up_b_hbm, conv_hbm, conv_b_hbm,
                    octs_ref, near_out, up_out, conv_out, bias_out,
                    children_ref, near_v, feat_ref, up_ref, up_b, conv_ref, conv_b,
                    table, slots, source_v, source, from_next, from_prev, low_own, high_own, halo_next, halo_prev,
                    near_pad, near_next, near_prev, send_sem, recv_sem, fetch_sem, feat_sem):
    columns = lax.axis_size("col")
    ranks = lax.axis_size("row") * columns
    rank = lax.axis_index("row") * columns + lax.axis_index("col")
    exists = {-1: rank > 0, 1: rank < ranks - 1}

    def device(offset):
        other = lax.rem(rank + offset + ranks, ranks)
        return other // columns, lax.rem(other, columns)

    barrier = pltpu.get_barrier_semaphore()
    for offset in (1, -1):
        @pl.when(exists[offset])
        def _(offset=offset):
            pl.semaphore_signal(barrier, inc=1, device_id=device(offset), device_id_type=pl.DeviceIdType.MESH)

    fetches = [pltpu.make_async_copy(src, dst, fetch_sem.at[number]) for number, (src, dst) in enumerate((
        (children_hbm, children_ref), (near_hbm, near_v), (up_hbm, up_ref), (conv_hbm, conv_ref),
        (up_b_hbm, up_b), (conv_b_hbm, conv_b)))]

    def feat_fetch(step):
        part = pl.ds(step * PACK, PACK)
        return pltpu.make_async_copy(feat_hbm.at[part], feat_ref.at[part], feat_sem.at[step])

    fetches[0].start()
    for step in range(12 // PACK):
        feat_fetch(step).start()
    for fetch in fetches[1:]:
        fetch.start()

    fetches[0].wait()
    slot_id = iota((8, 128), 0) * 128 + iota((8, 128), 1)
    first = (rank - 1) * OWN
    chosen = jnp.full((8, 128), 96, jnp.int32)
    for c in range(12):
        for o in range(8):
            child = children_ref[o, c]
            position = jnp.where(child >= 0, child - first, REACH)
            chosen = jnp.where(slot_id == position, 8 * c + o, chosen)
    source_v[...] = chosen
    source_copy = pltpu.make_async_copy(source_v, source, fetch_sem.at[6])
    source_copy.start()

    low_lane = iota((64, 128), 1) < 64
    low_row = iota((8, 128), 0) < 4
    table[96] = jnp.zeros((16, 256), BF16)

    def turn(c, pair):
        near = feat_ref[c, :, 128 * pair:128 * pair + 128].astype(F32)
        far = feat_ref[c, :, 256 + 128 * pair:384 + 128 * pair].astype(F32)
        top = jnp.where(low_lane, near, pltpu.roll(far, 64, 1))
        bottom = jnp.where(low_lane, pltpu.roll(near, 64, 1), far)
        return jnp.concatenate([top, bottom], axis=0).T

    def octants_of(turned):
        listed = []
        for octant in range(8):
            ox, oy, oz = octant // 4, octant // 2 % 2, octant % 2
            sheets = []
            for y in range(4):
                at = 64 * ox + 8 * (4 * oy + y)
                sheets.append(turned[at:at + 8])
            halves = []
            for one, two in ((sheets[0], sheets[1]), (sheets[2], sheets[3])):
                if oz == 0:
                    halves.append(jnp.where(low_row, one, pltpu.roll(two, 4, 0)))
                else:
                    halves.append(jnp.where(low_row, pltpu.roll(one, 4, 0), two))
            listed.append(jnp.concatenate(halves, axis=0).astype(BF16))
        return listed

    def coarse_blocks(step, _):
        feat_fetch(step).wait()
        turned = [[turn(step * PACK + k, pair) for pair in range(2)] for k in range(PACK)]
        for k in range(PACK):
            for pair in range(2):
                for octant, value in enumerate(octants_of(turned[k][pair])):
                    table[(step * PACK + k) * 8 + octant, :, 128 * pair:128 * pair + 128] = value
        return 0

    lax.fori_loop(0, 12 // PACK, coarse_blocks, 0)
    source_copy.wait()
    fetches[1].wait()
    near_pad[...] = jnp.zeros((32, 128), jnp.int32)
    near_pad[0:26, 0:48] = near_v[...]

    def octant_at(q):
        return table[source[q // 128, q % 128]]

    def fill(start, q_start):
        def body(k, _):
            for j in range(8):
                slots[start + k * 8 + j] = octant_at(q_start + k * 8 + j)
            return 0
        lax.fori_loop(0, OWN // 16, body, 0)

    half = OWN // 2
    plan = [
        (slots.at[0:half], from_next.at[0:half], -1),
        (slots.at[OWN:OWN + half], from_prev.at[0:half], 1),
        (slots.at[half:OWN], from_next.at[half:OWN], -1),
        (slots.at[OWN + half:2 * OWN], from_prev.at[half:OWN], 1),
        (near_pad, near_next, -1),
        (near_pad, near_prev, 1),
        (low_own, halo_next, -1),
        (high_own, halo_prev, 1),
    ]

    def transfer(number):
        src, dst, offset = plan[number]
        return pltpu.make_async_remote_copy(
            src_ref=src, dst_ref=dst, send_sem=send_sem.at[number], recv_sem=recv_sem.at[number],
            device_id=device(offset), device_id_type=pl.DeviceIdType.MESH)

    def send(*numbers):
        for number in numbers:
            @pl.when(exists[plan[number][2]])
            def _(number=number):
                transfer(number).start()

    def sent(*numbers):
        for number in numbers:
            @pl.when(exists[plan[number][2]])
            def _(number=number):
                transfer(number).wait_send()

    def landed(*numbers):
        for number in numbers:
            @pl.when(exists[-plan[number][2]])
            def _(number=number):
                transfer(number).wait_recv()

    for offset, refs, near in ((1, (from_next, halo_next), near_next), (-1, (from_prev, halo_prev), near_prev)):
        @pl.when(jnp.logical_not(exists[offset]))
        def _(refs=refs, near=near):
            for ref in refs:
                ref[...] = jnp.zeros(ref.shape, BF16)
            near[...] = jnp.full((32, 128), -1, jnp.int32)

    fill(0, 0)
    fill(OWN, 2 * OWN)
    pl.semaphore_wait(barrier, exists[1].astype(jnp.int32) + exists[-1].astype(jnp.int32))
    send(0, 1)
    fill(half, half)
    fill(OWN + half, 2 * OWN + half)
    send(2, 3, 4, 5)

    for fetch in fetches[2:]:
        fetch.wait()
    make_weights(up_ref, conv_ref, up_out, conv_out)
    spread = (iota((32, 256), 0) == iota((32, 256), 1) % 32).astype(F32)
    for number, ref in enumerate((up_b, conv_b)):
        bias_out[8 * number:8 * number + 8] = jnp.dot(
            jnp.broadcast_to(ref[...], (8, 32)), spread, precision=lax.Precision.HIGHEST,
            preferred_element_type=F32)
    octs_ref[SLOTS] = jnp.zeros((16, 256), F32)

    def join(start, stop, copy_ref, offset):
        def body(k, _):
            for j in range(4):
                b = start + k * 4 + j
                total = octant_at(OWN + b).astype(F32) + from_next[b].astype(F32) + from_prev[b].astype(F32)
                octs_ref[HALO + b] = total
                if copy_ref is not None:
                    copy_ref[b - offset] = total.astype(BF16)
            return 0
        lax.fori_loop(0, (stop - start) // 4, body, 0)

    landed(0, 1)
    join(0, half, low_own, 0)
    send(6)
    landed(2, 3)
    join(OWN - HALO, OWN, high_own, OWN - HALO)
    send(7)
    join(half, OWN - HALO, None, 0)
    landed(4, 5)
    lane = iota((32, 128), 1)
    near = jnp.where(lane < HALO, pltpu.roll(near_prev[...], 128 - (OWN - HALO), 1),
                     jnp.where(lane < HALO + OWN, pltpu.roll(near_pad[...], HALO, 1),
                               pltpu.roll(near_next[...], HALO + OWN, 1)))
    moved = near - (rank * OWN - HALO)
    near_out[...] = jnp.where((near >= 0) & (moved >= 0) & (moved < SLOTS), moved, SLOTS)
    landed(7)
    octs_ref[0:HALO] = halo_prev[...].astype(F32)
    landed(6)
    octs_ref[HALO + OWN:SLOTS] = halo_next[...].astype(F32)
    sent(*range(8))


def make_weights(up_ref, conv_ref, up_out, conv_out):
    spread = (iota((32, 256), 0) == iota((32, 256), 1) % 32).astype(BF16)
    lane_x = iota((32, 256), 1) // 32
    zero = jnp.zeros((32, 256), F32)
    wide = lax.dot_general(conv_ref[...], spread, (((0,), (0,)), ((), ())), preferred_element_type=F32)

    def tap_of(kx, ky, kz):
        at = 32 * (9 * kx + 3 * ky + kz)
        return wide[at:at + 32]

    for ky in range(3):
        for kz in range(3):
            taps = [tap_of(kx, ky, kz) for kx in range(3)]
            for x in range(8):
                value = zero
                for kx in range(3):
                    value = jnp.where(lane_x == x + 1 - kx, taps[kx], value)
                at = 256 * (3 * ky + kz) + 32 * x
                conv_out[at:at + 32] = value.astype(BF16)
    pairs = [((0, 0), (0, 1)), ((1, 0), (1, 1)), ((2, 0), (2, 1)), ((0, 2), (1, 2)), ((2, 2), None)]
    for tile, (even, odd) in enumerate(pairs):
        at = EXTRA_AT + 128 * tile

        def beyond(tap):
            return zero if tap is None else jnp.where(lane_x == 7, tap_of(2, *tap), zero)

        def before(tap):
            return zero if tap is None else jnp.where(lane_x == 0, tap_of(0, *tap), zero)

        conv_out[at:at + 32] = beyond(even).astype(BF16)
        conv_out[at + 32:at + 64] = before(odd).astype(BF16)
        conv_out[at + 64:at + 96] = beyond(odd).astype(BF16)
        conv_out[at + 96:at + 128] = before(even).astype(BF16)

    lane_f = iota((64, 256), 1) // 32
    zero_up = jnp.zeros((64, 256), F32)

    def up_tap(kx, ky, kz):
        code = 9 * kx + 3 * ky + kz
        return jnp.dot(up_ref[:, 32 * code:32 * code + 32], spread, preferred_element_type=F32)

    for (_, low, high, taps_of), start in zip(CLASSES, class_starts):
        for shift, at_lane in SHIFT_AT.items():
            if not low <= at_lane < high:
                continue
            at = start + at_lane - low
            taps = [up_tap(kx, *taps_of[shift]) for kx in range(3)]
            for x in range(4):
                value = zero_up
                for kx in range(3):
                    value = jnp.where(lane_f == 2 * x + kx - 1, taps[kx], value)
                up_out[at + 64 * x:at + 64 * x + 64] = value.astype(BF16)
        for number, shift in enumerate(((0, 0), (0, 1), (1, 0), (1, 1))):
            at = start + HALO_AT - low + 64 * number
            value = zero_up
            if shift in taps_of:
                value = jnp.where(lane_f == 7, up_tap(0, *taps_of[shift]), zero_up)
            up_out[at:at + 64] = value.astype(BF16)


def main_kernel(near_ref, octs, up_w, conv_w, bias, out_hbm, shifted, hidden, patches_0, patches_1, out_ref, out_sem):
    def shift_z(value, beyond):
        last = iota(value.shape, 0) % 4 == 3
        return jnp.where(last, pltpu.roll(beyond, 3, 0), pltpu.roll(value, 15, 0))

    def shift_y(value, beyond):
        first = iota(value.shape, 0) < 4
        return pltpu.roll(jnp.where(first, beyond, value), 12, 0)

    low_lane16 = iota((16, 128), 1) < 64

    def spread_octant(h):
        at = [near_ref[column, h] for column in upward_columns]
        here, z_next, y_next, yz_next = octs[h], octs[at[0]], octs[at[1]], octs[at[2]]
        by_z = shift_z(here, z_next)
        x0, xz, xy, xyz = [octs[at[j], :, 0:128] for j in (3, 4, 5, 6)]
        x_by_z = shift_z(x0, xz)
        x_by_y = shift_y(x0, xy)
        x_by_yz = shift_y(x_by_z, shift_z(xy, xyz))
        return [
            (0, shift_y(here, y_next)),
            (256, jnp.where(low_lane16, x0, pltpu.roll(x_by_z, 64, 1))),
            (384, jnp.where(low_lane16, x_by_y, pltpu.roll(x_by_yz, 64, 1))),
            (512, here),
            (768, by_z),
            (1024, shift_y(by_z, shift_z(y_next, yz_next))),
        ]

    def spread_octants(group, _):
        for h, parts in [(group * SPREAD + k, spread_octant(group * SPREAD + k)) for k in range(SPREAD)]:
            for lane, value in parts:
                shifted[h, :, lane:lane + value.shape[1]] = value.astype(BF16)
        return 0

    lax.fori_loop(0, ACTIVE // SPREAD, spread_octants, 0)

    hidden[:, SLOTS] = jnp.zeros((2, 64, 128), F32)
    up_bias = bias[0:1]

    def upsample(chunk, _):
        for ((py, pz), low, high, _), start in zip(CLASSES, class_starts):
            rows = shifted[pl.ds(chunk * UP, UP), :, low:high].reshape(16 * UP, high - low)
            value = jnp.dot(rows, up_w[start:start + high - low], preferred_element_type=F32) + up_bias
            half = 0.5 * value
            value = half + half * jnp.tanh(half)
            for b in range(UP):
                for y in range(4):
                    part = value[16 * b + 4 * y:16 * b + 4 * y + 4]
                    for tile in range(2):
                        hidden[tile, chunk * UP + b, pl.ds(8 * (2 * y + py) + pz, 4, stride=2), :] = (
                            part[:, 128 * tile:128 * tile + 128])
        return 0

    lax.fori_loop(0, ACTIVE // UP, upsample, 0)

    conv_bias = bias[8:9]
    row = iota((8, 128), 0)
    first_row, last_row = row == 0, row == 7
    low_lane8 = iota((8, 128), 1) < 64
    lane = iota((8, 128), 1)
    even_lane = (lane < 32) | (lane >= 96)
    low_lane32 = iota((32, 128), 1) < 64

    def shift_row(dz, value, beyond):
        if dz == 0:
            return value
        if dz == 1:
            return pltpu.roll(jnp.where(first_row, beyond, value), 7, 0)
        return pltpu.roll(jnp.where(last_row, beyond, value), 1, 0)

    def two(one, other):
        return jnp.concatenate([one, other], axis=0).astype(BF16)

    def build(patches, b, k):
        at = {delta: near_ref[column, b + HALO] for delta, column in column_of.items()}
        at[(0, 0, 0)] = b + HALO

        def sheet(delta, y, tile):
            return hidden[tile, at[delta], 8 * y:8 * y + 8, :]

        def side(dy, dz, y):
            return jnp.where(low_lane8, sheet((1, dy, dz), y, 0), sheet((-1, dy, dz), y, 1))

        def sheets(dz, take):
            listed = []
            for step in range(10):
                dy = -1 if step == 0 else (1 if step == 9 else 0)
                y = (step - 1) % 8
                beyond = None if dz == 0 else take(dy, dz, y)
                listed.append(shift_row(dz, take(dy, 0, y), beyond))
            return listed

        def put(values, ky, at_lane):
            for pair in range(4):
                patches[k, 16 * pair:16 * pair + 16, at_lane:at_lane + 128] = values[pair]

        def put_all(listed, lanes):
            even = [two(listed[2 * n], listed[2 * n + 1]) for n in range(5)]
            odd = [two(listed[2 * n + 1], listed[2 * n + 2]) for n in range(4)]
            put(even[0:4], 0, lanes[0])
            put(odd, 1, lanes[1])
            put(even[1:5], 2, lanes[2])

        for dz in (-1, 0, 1):
            for tile in range(2):
                listed = sheets(dz, lambda dy, dz_, y: sheet((0, dy, dz_), y, tile))
                put_all(listed, [256 * (3 * ky + dz + 1) + 128 * tile for ky in range(3)])
        sides = [sheets(dz, side) for dz in (-1, 0, 1)]
        joined = [jnp.where(even_lane, one, pltpu.roll(other, 64, 1)) for one, other in zip(sides[0], sides[1])]
        put_all(joined, [EXTRA_AT + 128 * ky for ky in range(3)])
        last = sides[2]
        paired = [jnp.where(even_lane, last[n], pltpu.roll(last[n + 1], 64, 1)) for n in range(8)]
        put([two(paired[2 * n], paired[2 * n + 1]) for n in range(4)], 0, EXTRA_AT + 384)
        put([two(last[2 * n + 2], last[2 * n + 3]) for n in range(4)], 0, EXTRA_AT + 512)

    def convolve(patches, base):
        value = jnp.dot(patches[...].reshape(64 * GROUP, CONV_K), conv_w[...], preferred_element_type=F32) + conv_bias
        for pair in range(GROUP // 2):
            for half in range(2):
                turned = value[128 * pair:128 * pair + 128, 128 * half:128 * half + 128].T
                for x in range(0, 4, 2):
                    one, other = turned[32 * x:32 * x + 32], turned[32 * x + 32:32 * x + 64]
                    at = 256 * half + 64 * x
                    b = base + 2 * pair
                    out_ref[b, :, at:at + 128] = jnp.where(
                        low_lane32, one, pltpu.roll(other, 64, 1)).astype(BF16)
                    out_ref[b + 1, :, at:at + 128] = jnp.where(
                        low_lane32, pltpu.roll(one, 64, 1), other).astype(BF16)

    def build_group(patches, base):
        for k in range(GROUP):
            build(patches, base + k, k)

    def write_out(step):
        part = pl.ds(step * 2 * GROUP, 2 * GROUP)
        return pltpu.make_async_copy(out_ref.at[part], out_hbm.at[part], out_sem.at[step])

    build_group(patches_0, 0)

    def groups(step, _):
        base = step * 2 * GROUP
        build_group(patches_1, base + GROUP)
        convolve(patches_0, base)
        build_group(patches_0, jnp.minimum(base + 2 * GROUP, OWN - GROUP))
        convolve(patches_1, base + GROUP)
        write_out(step).start()
        return 0

    lax.fori_loop(0, OWN // (2 * GROUP), groups, 0)
    for step in range(OWN // (2 * GROUP)):
        write_out(step).wait()


VMEM = pl.BlockSpec(memory_space=pltpu.VMEM)
SMEM = pl.BlockSpec(memory_space=pltpu.SMEM)
ANY = pl.BlockSpec(memory_space=pltpu.MemorySpace.HBM)


def in_hbm(array):
    return pltpu.with_memory_space_constraint(array, pltpu.HBM)


def on_device(
    coarse_feat, coarse_children, fine_neighbours, up_weight, up_bias, conv_weight, conv_bias
):
    octs, near, up_w, conv_w, bias = pl.pallas_call(
        exchange_kernel,
        out_shape=[
            jax.ShapeDtypeStruct((SLOTS + 1, 16, 256), F32),
            jax.ShapeDtypeStruct((32, 128), jnp.int32),
            jax.ShapeDtypeStruct((UP_K, 256), BF16),
            jax.ShapeDtypeStruct((CONV_K, 256), BF16),
            jax.ShapeDtypeStruct((16, 256), F32),
        ],
        in_specs=[ANY] * 7,
        out_specs=[VMEM] * 5,
        scratch_shapes=[
            pltpu.SMEM((8, 12), jnp.int32),
            pltpu.VMEM((26, OWN), jnp.int32),
            pltpu.VMEM((12, 64, 512), BF16),
            pltpu.VMEM((64, 864), BF16),
            pltpu.VMEM((1, 32), F32),
            pltpu.VMEM((32, 864), BF16),
            pltpu.VMEM((1, 32), F32),
            pltpu.VMEM((97, 16, 256), BF16),
            pltpu.VMEM((2 * OWN, 16, 256), BF16),
            pltpu.VMEM((8, 128), jnp.int32),
            pltpu.SMEM((8, 128), jnp.int32),
            pltpu.VMEM((OWN, 16, 256), BF16),
            pltpu.VMEM((OWN, 16, 256), BF16),
            pltpu.VMEM((2 * HALO, 16, 256), BF16),
            pltpu.VMEM((HALO, 16, 256), BF16),
            pltpu.VMEM((2 * HALO, 16, 256), BF16),
            pltpu.VMEM((HALO, 16, 256), BF16),
            pltpu.VMEM((32, 128), jnp.int32),
            pltpu.VMEM((32, 128), jnp.int32),
            pltpu.VMEM((32, 128), jnp.int32),
            pltpu.SemaphoreType.DMA((8,)),
            pltpu.SemaphoreType.DMA((8,)),
            pltpu.SemaphoreType.DMA((7,)),
            pltpu.SemaphoreType.DMA((12 // PACK,)),
        ],
        compiler_params=pltpu.CompilerParams(
            vmem_limit_bytes=40 * 2 ** 20, collective_id=0, has_side_effects=True),
        name="exchange",
    )(*[in_hbm(x) for x in (
        coarse_children.T, fine_neighbours.T, coarse_feat, up_weight, up_bias[None, :], conv_weight, conv_bias[None, :])])
    return pl.pallas_call(
        main_kernel,
        out_shape=jax.ShapeDtypeStruct((OWN, 32, 512), BF16),
        in_specs=[SMEM, VMEM, VMEM, VMEM, VMEM],
        out_specs=ANY,
        scratch_shapes=[
            pltpu.VMEM((ACTIVE, 16, 1280), BF16),
            pltpu.VMEM((2, SLOTS + 1, 64, 128), F32),
            pltpu.VMEM((GROUP, 64, CONV_K), BF16),
            pltpu.VMEM((GROUP, 64, CONV_K), BF16),
            pltpu.VMEM((OWN, 32, 512), BF16),
            pltpu.SemaphoreType.DMA((OWN // (2 * GROUP),)),
        ],
        compiler_params=pltpu.CompilerParams(vmem_limit_bytes=48 * 2 ** 20),
        name="convolutions",
    )(near, octs, up_w, conv_w, bias)


def solution(mesh):
    in_specs = (
        P(AXES, None, None),
        P(AXES, None),
        P(AXES, None),
        P(),
        P(),
        P(),
        P(),
    )
    return jax.shard_map(
        on_device, mesh=mesh, in_specs=in_specs, out_specs=P(AXES, None, None), check_vma=False
    )
```

```python
import jax
import jax.numpy as jnp
from jax import lax
from jax.experimental import pallas as pl
from jax.experimental.pallas import tpu as pltpu
from jax.sharding import PartitionSpec as P

F32 = jnp.float32
BF16 = jnp.bfloat16
AXES = ("row", "col")
HALO = 12
OWN = 48
SLOTS = OWN + 3 * HALO
ACTIVE = OWN + 2 * HALO
REACH = 3 * OWN
PACK = 3
SPREAD = 6
GROUP = 6
INNER = OWN - HALO
EXTRA_AT = 9 * 256
CONV_K = EXTRA_AT + 5 * 128

direction_list = [
    (code // 9 - 1, code // 3 % 3 - 1, code % 3 - 1) for code in range(27) if code != 13
]
column_of = {delta: column for column, delta in enumerate(direction_list)}
upward_list = [(0, 0, 1), (0, 1, 0), (0, 1, 1), (1, 0, 0), (1, 0, 1), (1, 1, 0), (1, 1, 1)]
upward_columns = [column_of[delta] for delta in upward_list]

CLASSES = [
    ((0, 0), 256, 1024 - 256, {(0, 0): (1, 1)}),
    ((0, 1), 256, 1024, {(0, 0): (1, 2), (0, 1): (1, 0)}),
    ((1, 0), 0, 768, {(0, 0): (2, 1), (1, 0): (0, 1)}),
    ((1, 1), 0, 1280, {(0, 0): (2, 2), (0, 1): (2, 0), (1, 0): (0, 2), (1, 1): (0, 0)}),
]
SHIFT_AT = {(1, 0): 0, (0, 0): 512, (0, 1): 768, (1, 1): 1024}
HALO_AT = 256
class_starts = []
UP_K = 0
for _, low, high, _ in CLASSES:
    class_starts.append(UP_K)
    UP_K += high - low


def iota(shape, dim):
    return lax.broadcasted_iota(jnp.int32, shape, dim)


def exchange_kernel(children_hbm, near_hbm, feat_hbm, up_hbm, up_b_hbm, conv_hbm, conv_b_hbm,
                    octs_ref, near_out, up_out, conv_out, bias_out, inner_hidden, inner_out,
                    children_ref, near_v, feat_ref, up_ref, up_b, conv_ref, conv_b,
                    table, slots, source_v, source, from_next, from_prev, low_own, high_own, halo_next, halo_prev,
                    near_pad, near_next, near_prev, inner_near_v, inner_near, shifted, patches_0, patches_1,
                    send_sem, recv_sem, fetch_sem, feat_sem):
    columns = lax.axis_size("col")
    ranks = lax.axis_size("row") * columns
    rank = lax.axis_index("row") * columns + lax.axis_index("col")
    exists = {-1: rank > 0, 1: rank < ranks - 1}

    def device(offset):
        other = lax.rem(rank + offset + ranks, ranks)
        return other // columns, lax.rem(other, columns)

    barrier = pltpu.get_barrier_semaphore()
    for offset in (1, -1):
        @pl.when(exists[offset])
        def _(offset=offset):
            pl.semaphore_signal(barrier, inc=1, device_id=device(offset), device_id_type=pl.DeviceIdType.MESH)

    fetches = [pltpu.make_async_copy(src, dst, fetch_sem.at[number]) for number, (src, dst) in enumerate((
        (children_hbm, children_ref), (near_hbm, near_v), (up_hbm, up_ref), (conv_hbm, conv_ref),
        (up_b_hbm, up_b), (conv_b_hbm, conv_b)))]

    def feat_fetch(step):
        part = pl.ds(step * PACK, PACK)
        return pltpu.make_async_copy(feat_hbm.at[part], feat_ref.at[part], feat_sem.at[step])

    fetches[0].start()
    for step in range(12 // PACK):
        feat_fetch(step).start()
    for fetch in fetches[1:]:
        fetch.start()

    fetches[0].wait()
    slot_id = iota((8, 128), 0) * 128 + iota((8, 128), 1)
    first = (rank - 1) * OWN
    chosen = jnp.full((8, 128), 96, jnp.int32)
    for c in range(12):
        for o in range(8):
            child = children_ref[o, c]
            position = jnp.where(child >= 0, child - first, REACH)
            chosen = jnp.where(slot_id == position, 8 * c + o, chosen)
    source_v[...] = chosen
    source_copy = pltpu.make_async_copy(source_v, source, fetch_sem.at[6])
    source_copy.start()

    low_lane = iota((64, 128), 1) < 64
    low_row = iota((8, 128), 0) < 4
    table[96] = jnp.zeros((16, 256), BF16)

    def turn(c, pair):
        near = feat_ref[c, :, 128 * pair:128 * pair + 128].astype(F32)
        far = feat_ref[c, :, 256 + 128 * pair:384 + 128 * pair].astype(F32)
        top = jnp.where(low_lane, near, pltpu.roll(far, 64, 1))
        bottom = jnp.where(low_lane, pltpu.roll(near, 64, 1), far)
        return jnp.concatenate([top, bottom], axis=0).T

    def octants_of(turned):
        listed = []
        for octant in range(8):
            ox, oy, oz = octant // 4, octant // 2 % 2, octant % 2
            sheets = []
            for y in range(4):
                at = 64 * ox + 8 * (4 * oy + y)
                sheets.append(turned[at:at + 8])
            halves = []
            for one, two in ((sheets[0], sheets[1]), (sheets[2], sheets[3])):
                if oz == 0:
                    halves.append(jnp.where(low_row, one, pltpu.roll(two, 4, 0)))
                else:
                    halves.append(jnp.where(low_row, pltpu.roll(one, 4, 0), two))
            listed.append(jnp.concatenate(halves, axis=0).astype(BF16))
        return listed

    def coarse_blocks(step, _):
        feat_fetch(step).wait()
        turned = [[turn(step * PACK + k, pair) for pair in range(2)] for k in range(PACK)]
        for k in range(PACK):
            for pair in range(2):
                for octant, value in enumerate(octants_of(turned[k][pair])):
                    table[(step * PACK + k) * 8 + octant, :, 128 * pair:128 * pair + 128] = value
        return 0

    lax.fori_loop(0, 12 // PACK, coarse_blocks, 0)
    source_copy.wait()
    fetches[1].wait()
    near_pad[...] = jnp.zeros((32, 128), jnp.int32)
    near_pad[0:26, 0:48] = near_v[...]
    inside = near_pad[...] - rank * OWN
    within = (near_pad[...] >= 0) & (inside >= 0) & (inside < OWN)
    inner_near_v[0:32] = jnp.where(within, inside + HALO, SLOTS)
    inner_near_v[32:64] = jnp.where(within & (inside < INNER), inside, INNER)
    inner_copy = pltpu.make_async_copy(inner_near_v, inner_near, fetch_sem.at[7])
    inner_copy.start()

    def octant_at(q):
        return table[source[q // 128, q % 128]]

    def fill(start, q_start):
        def body(k, _):
            for j in range(8):
                slots[start + k * 8 + j] = octant_at(q_start + k * 8 + j)
            return 0
        lax.fori_loop(0, OWN // 16, body, 0)

    half = OWN // 2
    plan = [
        (slots.at[0:half], from_next.at[0:half], -1),
        (slots.at[OWN:OWN + half], from_prev.at[0:half], 1),
        (slots.at[half:OWN], from_next.at[half:OWN], -1),
        (slots.at[OWN + half:2 * OWN], from_prev.at[half:OWN], 1),
        (near_pad, near_next, -1),
        (near_pad, near_prev, 1),
        (low_own, halo_next, -1),
        (high_own, halo_prev, 1),
    ]

    def transfer(number):
        src, dst, offset = plan[number]
        return pltpu.make_async_remote_copy(
            src_ref=src, dst_ref=dst, send_sem=send_sem.at[number], recv_sem=recv_sem.at[number],
            device_id=device(offset), device_id_type=pl.DeviceIdType.MESH)

    def send(*numbers):
        for number in numbers:
            @pl.when(exists[plan[number][2]])
            def _(number=number):
                transfer(number).start()

    def sent(*numbers):
        for number in numbers:
            @pl.when(exists[plan[number][2]])
            def _(number=number):
                transfer(number).wait_send()

    def landed(*numbers):
        for number in numbers:
            @pl.when(exists[-plan[number][2]])
            def _(number=number):
                transfer(number).wait_recv()

    for offset, refs, near in ((1, (from_next, halo_next), near_next), (-1, (from_prev, halo_prev), near_prev)):
        @pl.when(jnp.logical_not(exists[offset]))
        def _(refs=refs, near=near):
            for ref in refs:
                ref[...] = jnp.zeros(ref.shape, BF16)
            near[...] = jnp.full((32, 128), -1, jnp.int32)

    fill(0, 0)
    fill(OWN, 2 * OWN)
    pl.semaphore_wait(barrier, exists[1].astype(jnp.int32) + exists[-1].astype(jnp.int32))
    send(0, 1)
    fill(half, half)
    fill(OWN + half, 2 * OWN + half)
    send(2, 3, 4, 5)

    for fetch in fetches[2:]:
        fetch.wait()
    make_weights(up_ref, conv_ref, up_out, conv_out)
    spread = (iota((32, 256), 0) == iota((32, 256), 1) % 32).astype(F32)
    for number, ref in enumerate((up_b, conv_b)):
        bias_out[8 * number:8 * number + 8] = jnp.dot(
            jnp.broadcast_to(ref[...], (8, 32)), spread, precision=lax.Precision.HIGHEST,
            preferred_element_type=F32)
    octs_ref[SLOTS] = jnp.zeros((16, 256), F32)
    inner_hidden[:, INNER] = jnp.zeros((2, 64, 128), F32)
    inner_copy.wait()

    def join(start, stop, copy_ref, offset):
        def body(k, _):
            for j in range(4):
                b = start + k * 4 + j
                total = octant_at(OWN + b).astype(F32) + from_next[b].astype(F32) + from_prev[b].astype(F32)
                octs_ref[HALO + b] = total
                if copy_ref is not None:
                    copy_ref[b - offset] = total.astype(BF16)
            return 0
        lax.fori_loop(0, (stop - start) // 4, body, 0)

    landed(0, 1)
    join(0, half, low_own, 0)
    send(6)
    landed(2, 3)
    join(OWN - HALO, OWN, high_own, OWN - HALO)
    send(7)
    join(half, OWN - HALO, None, 0)

    spread_octants(inner_near, octs_ref, shifted, HALO, 0, INNER)
    up_bias = bias_out[0:1]

    def inner_upsample(chunk, _):
        upsample(shifted, up_out, up_bias, inner_hidden, chunk * (INNER // 2), INNER // 2)
        return 0

    lax.fori_loop(0, 2, inner_upsample, 0)
    build_group, convolve = convolver(
        lambda column, b: inner_near[32 + column, b], 0, inner_hidden, conv_out, bias_out[8:9], inner_out, HALO)
    build_group(patches_0, HALO)
    build_group(patches_1, HALO + GROUP)
    convolve(patches_0, HALO)
    convolve(patches_1, HALO + GROUP)
    landed(4, 5)
    lane = iota((32, 128), 1)
    near = jnp.where(lane < HALO, pltpu.roll(near_prev[...], 128 - (OWN - HALO), 1),
                     jnp.where(lane < HALO + OWN, pltpu.roll(near_pad[...], HALO, 1),
                               pltpu.roll(near_next[...], HALO + OWN, 1)))
    moved = near - (rank * OWN - HALO)
    near_out[...] = jnp.where((near >= 0) & (moved >= 0) & (moved < SLOTS), moved, SLOTS)
    landed(7)
    octs_ref[0:HALO] = halo_prev[...].astype(F32)
    landed(6)
    octs_ref[HALO + OWN:SLOTS] = halo_next[...].astype(F32)
    sent(*range(8))


def make_weights(up_ref, conv_ref, up_out, conv_out):
    spread = (iota((32, 256), 0) == iota((32, 256), 1) % 32).astype(BF16)
    lane_x = iota((32, 256), 1) // 32
    zero = jnp.zeros((32, 256), F32)
    wide = lax.dot_general(conv_ref[...], spread, (((0,), (0,)), ((), ())), preferred_element_type=F32)

    def tap_of(kx, ky, kz):
        at = 32 * (9 * kx + 3 * ky + kz)
        return wide[at:at + 32]

    for ky in range(3):
        for kz in range(3):
            taps = [tap_of(kx, ky, kz) for kx in range(3)]
            for x in range(8):
                value = zero
                for kx in range(3):
                    value = jnp.where(lane_x == x + 1 - kx, taps[kx], value)
                at = 256 * (3 * ky + kz) + 32 * x
                conv_out[at:at + 32] = value.astype(BF16)
    pairs = [((0, 0), (0, 1)), ((1, 0), (1, 1)), ((2, 0), (2, 1)), ((0, 2), (1, 2)), ((2, 2), None)]
    for tile, (even, odd) in enumerate(pairs):
        at = EXTRA_AT + 128 * tile

        def beyond(tap):
            return zero if tap is None else jnp.where(lane_x == 7, tap_of(2, *tap), zero)

        def before(tap):
            return zero if tap is None else jnp.where(lane_x == 0, tap_of(0, *tap), zero)

        conv_out[at:at + 32] = beyond(even).astype(BF16)
        conv_out[at + 32:at + 64] = before(odd).astype(BF16)
        conv_out[at + 64:at + 96] = beyond(odd).astype(BF16)
        conv_out[at + 96:at + 128] = before(even).astype(BF16)

    lane_f = iota((64, 256), 1) // 32
    zero_up = jnp.zeros((64, 256), F32)

    def up_tap(kx, ky, kz):
        code = 9 * kx + 3 * ky + kz
        return jnp.dot(up_ref[:, 32 * code:32 * code + 32], spread, preferred_element_type=F32)

    for (_, low, high, taps_of), start in zip(CLASSES, class_starts):
        for shift, at_lane in SHIFT_AT.items():
            if not low <= at_lane < high:
                continue
            at = start + at_lane - low
            taps = [up_tap(kx, *taps_of[shift]) for kx in range(3)]
            for x in range(4):
                value = zero_up
                for kx in range(3):
                    value = jnp.where(lane_f == 2 * x + kx - 1, taps[kx], value)
                up_out[at + 64 * x:at + 64 * x + 64] = value.astype(BF16)
        for number, shift in enumerate(((0, 0), (0, 1), (1, 0), (1, 1))):
            at = start + HALO_AT - low + 64 * number
            value = zero_up
            if shift in taps_of:
                value = jnp.where(lane_f == 7, up_tap(0, *taps_of[shift]), zero_up)
            up_out[at:at + 64] = value.astype(BF16)


def spread_octants(near_ref, octs, shifted, offset, start, stop):
    def shift_z(value, beyond):
        last = iota(value.shape, 0) % 4 == 3
        return jnp.where(last, pltpu.roll(beyond, 3, 0), pltpu.roll(value, 15, 0))

    def shift_y(value, beyond):
        first = iota(value.shape, 0) < 4
        return pltpu.roll(jnp.where(first, beyond, value), 12, 0)

    low_lane16 = iota((16, 128), 1) < 64

    def spread_octant(h):
        at = [near_ref[column, h] for column in upward_columns]
        here, z_next, y_next, yz_next = octs[h + offset], octs[at[0]], octs[at[1]], octs[at[2]]
        by_z = shift_z(here, z_next)
        x0, xz, xy, xyz = [octs[at[j], :, 0:128] for j in (3, 4, 5, 6)]
        x_by_z = shift_z(x0, xz)
        x_by_y = shift_y(x0, xy)
        x_by_yz = shift_y(x_by_z, shift_z(xy, xyz))
        return [
            (0, shift_y(here, y_next)),
            (256, jnp.where(low_lane16, x0, pltpu.roll(x_by_z, 64, 1))),
            (384, jnp.where(low_lane16, x_by_y, pltpu.roll(x_by_yz, 64, 1))),
            (512, here),
            (768, by_z),
            (1024, shift_y(by_z, shift_z(y_next, yz_next))),
        ]

    def group_of(group, _):
        for h, parts in [(group * SPREAD + k, spread_octant(group * SPREAD + k)) for k in range(SPREAD)]:
            for lane, value in parts:
                shifted[h, :, lane:lane + value.shape[1]] = value.astype(BF16)
        return 0

    lax.fori_loop(start // SPREAD, stop // SPREAD, group_of, 0)


def upsample(shifted, up_w, up_bias, hidden, start, count):
    for ((py, pz), low, high, _), at in zip(CLASSES, class_starts):
        rows = shifted[pl.ds(start, count), :, low:high].reshape(16 * count, high - low)
        value = jnp.dot(rows, up_w[at:at + high - low], preferred_element_type=F32) + up_bias
        half = 0.5 * value
        value = half + half * jnp.tanh(half)
        for b in range(count):
            for y in range(4):
                part = value[16 * b + 4 * y:16 * b + 4 * y + 4]
                for tile in range(2):
                    hidden[tile, start + b, pl.ds(8 * (2 * y + py) + pz, 4, stride=2), :] = (
                        part[:, 128 * tile:128 * tile + 128])


def convolver(nearby, offset, hidden, conv_w, conv_bias, out_ref, out_offset):
    row = iota((8, 128), 0)
    first_row, last_row = row == 0, row == 7
    low_lane8 = iota((8, 128), 1) < 64
    lane = iota((8, 128), 1)
    even_lane = (lane < 32) | (lane >= 96)
    low_lane32 = iota((32, 128), 1) < 64

    def shift_row(dz, value, beyond):
        if dz == 0:
            return value
        if dz == 1:
            return pltpu.roll(jnp.where(first_row, beyond, value), 7, 0)
        return pltpu.roll(jnp.where(last_row, beyond, value), 1, 0)

    def two(one, other):
        return jnp.concatenate([one, other], axis=0).astype(BF16)

    def build(patches, b, k):
        at = {delta: nearby(column, b) for delta, column in column_of.items()}
        at[(0, 0, 0)] = b + offset

        def sheet(delta, y, tile):
            return hidden[tile, at[delta], 8 * y:8 * y + 8, :]

        def side(dy, dz, y):
            return jnp.where(low_lane8, sheet((1, dy, dz), y, 0), sheet((-1, dy, dz), y, 1))

        def sheets(dz, take):
            listed = []
            for step in range(10):
                dy = -1 if step == 0 else (1 if step == 9 else 0)
                y = (step - 1) % 8
                beyond = None if dz == 0 else take(dy, dz, y)
                listed.append(shift_row(dz, take(dy, 0, y), beyond))
            return listed

        def put(values, ky, at_lane):
            for pair in range(4):
                patches[k, 16 * pair:16 * pair + 16, at_lane:at_lane + 128] = values[pair]

        def put_all(listed, lanes):
            even = [two(listed[2 * n], listed[2 * n + 1]) for n in range(5)]
            odd = [two(listed[2 * n + 1], listed[2 * n + 2]) for n in range(4)]
            put(even[0:4], 0, lanes[0])
            put(odd, 1, lanes[1])
            put(even[1:5], 2, lanes[2])

        for dz in (-1, 0, 1):
            for tile in range(2):
                listed = sheets(dz, lambda dy, dz_, y: sheet((0, dy, dz_), y, tile))
                put_all(listed, [256 * (3 * ky + dz + 1) + 128 * tile for ky in range(3)])
        sides = [sheets(dz, side) for dz in (-1, 0, 1)]
        joined = [jnp.where(even_lane, one, pltpu.roll(other, 64, 1)) for one, other in zip(sides[0], sides[1])]
        put_all(joined, [EXTRA_AT + 128 * ky for ky in range(3)])
        last = sides[2]
        paired = [jnp.where(even_lane, last[n], pltpu.roll(last[n + 1], 64, 1)) for n in range(8)]
        put([two(paired[2 * n], paired[2 * n + 1]) for n in range(4)], 0, EXTRA_AT + 384)
        put([two(last[2 * n + 2], last[2 * n + 3]) for n in range(4)], 0, EXTRA_AT + 512)

    def convolve(patches, base):
        value = jnp.dot(patches[...].reshape(64 * GROUP, CONV_K), conv_w[...], preferred_element_type=F32) + conv_bias
        for pair in range(GROUP // 2):
            for half in range(2):
                turned = value[128 * pair:128 * pair + 128, 128 * half:128 * half + 128].T
                for x in range(0, 4, 2):
                    one, other = turned[32 * x:32 * x + 32], turned[32 * x + 32:32 * x + 64]
                    at = 256 * half + 64 * x
                    b = base + 2 * pair
                    out_ref[b - out_offset, :, at:at + 128] = jnp.where(
                        low_lane32, one, pltpu.roll(other, 64, 1)).astype(BF16)
                    out_ref[b + 1 - out_offset, :, at:at + 128] = jnp.where(
                        low_lane32, pltpu.roll(one, 64, 1), other).astype(BF16)

    def build_group(patches, base):
        for k in range(GROUP):
            build(patches, base + k, k)

    return build_group, convolve


def main_kernel(near_ref, octs, up_w, conv_w, bias, inner_hidden, inner_out, out_hbm,
                shifted, hidden, patches_0, patches_1, out_ref, out_sem, inner_sem):
    bring = pltpu.make_async_copy(inner_hidden.at[:, 0:INNER], hidden.at[:, HALO:HALO + INNER], inner_sem.at[0])
    bring.start()
    middle = pltpu.make_async_copy(inner_out, out_hbm.at[HALO:2 * HALO], inner_sem.at[1])
    middle.start()
    hidden[:, SLOTS] = jnp.zeros((2, 64, 128), F32)
    spread_octants(near_ref, octs, shifted, 0, 0, HALO)
    spread_octants(near_ref, octs, shifted, 0, HALO + INNER, ACTIVE)
    up_bias = bias[0:1]
    upsample(shifted, up_w, up_bias, hidden, 0, HALO)
    upsample(shifted, up_w, up_bias, hidden, HALO + INNER, 2 * HALO)
    bring.wait()

    build_group, convolve = convolver(
        lambda column, b: near_ref[column, b + HALO], HALO, hidden, conv_w, bias[8:9], out_ref, 0)

    def base_of(step):
        return jnp.where(step > 0, 2 * GROUP * (step + 1), 0)

    def write_out(step):
        part = pl.ds(base_of(step), 2 * GROUP)
        return pltpu.make_async_copy(out_ref.at[part], out_hbm.at[part], out_sem.at[step])

    build_group(patches_0, 0)

    def groups(step, _):
        base = base_of(step)
        build_group(patches_1, base + GROUP)
        convolve(patches_0, base)
        build_group(patches_0, base_of(jnp.minimum(step + 1, 2)))
        convolve(patches_1, base + GROUP)
        write_out(step).start()
        return 0

    lax.fori_loop(0, 3, groups, 0)
    middle.wait()
    for step in range(3):
        write_out(step).wait()


VMEM = pl.BlockSpec(memory_space=pltpu.VMEM)
SMEM = pl.BlockSpec(memory_space=pltpu.SMEM)
ANY = pl.BlockSpec(memory_space=pltpu.MemorySpace.HBM)


def in_hbm(array):
    return pltpu.with_memory_space_constraint(array, pltpu.HBM)


def on_device(
    coarse_feat, coarse_children, fine_neighbours, up_weight, up_bias, conv_weight, conv_bias
):
    octs, near, up_w, conv_w, bias, inner_hidden, inner_out = pl.pallas_call(
        exchange_kernel,
        out_shape=[
            jax.ShapeDtypeStruct((SLOTS + 1, 16, 256), F32),
            jax.ShapeDtypeStruct((32, 128), jnp.int32),
            jax.ShapeDtypeStruct((UP_K, 256), BF16),
            jax.ShapeDtypeStruct((CONV_K, 256), BF16),
            jax.ShapeDtypeStruct((16, 256), F32),
            jax.ShapeDtypeStruct((2, INNER + 1, 64, 128), F32),
            jax.ShapeDtypeStruct((HALO, 32, 512), BF16),
        ],
        in_specs=[ANY] * 7,
        out_specs=[VMEM] * 7,
        scratch_shapes=[
            pltpu.SMEM((8, 12), jnp.int32),
            pltpu.VMEM((26, OWN), jnp.int32),
            pltpu.VMEM((12, 64, 512), BF16),
            pltpu.VMEM((64, 864), BF16),
            pltpu.VMEM((1, 32), F32),
            pltpu.VMEM((32, 864), BF16),
            pltpu.VMEM((1, 32), F32),
            pltpu.VMEM((97, 16, 256), BF16),
            pltpu.VMEM((2 * OWN, 16, 256), BF16),
            pltpu.VMEM((8, 128), jnp.int32),
            pltpu.SMEM((8, 128), jnp.int32),
            pltpu.VMEM((OWN, 16, 256), BF16),
            pltpu.VMEM((OWN, 16, 256), BF16),
            pltpu.VMEM((2 * HALO, 16, 256), BF16),
            pltpu.VMEM((HALO, 16, 256), BF16),
            pltpu.VMEM((2 * HALO, 16, 256), BF16),
            pltpu.VMEM((HALO, 16, 256), BF16),
            pltpu.VMEM((32, 128), jnp.int32),
            pltpu.VMEM((32, 128), jnp.int32),
            pltpu.VMEM((32, 128), jnp.int32),
            pltpu.VMEM((64, 128), jnp.int32),
            pltpu.SMEM((64, 128), jnp.int32),
            pltpu.VMEM((INNER, 16, 1280), BF16),
            pltpu.VMEM((GROUP, 64, CONV_K), BF16),
            pltpu.VMEM((GROUP, 64, CONV_K), BF16),
            pltpu.SemaphoreType.DMA((8,)),
            pltpu.SemaphoreType.DMA((8,)),
            pltpu.SemaphoreType.DMA((8,)),
            pltpu.SemaphoreType.DMA((12 // PACK,)),
        ],
        compiler_params=pltpu.CompilerParams(
            vmem_limit_bytes=32 * 2 ** 20, collective_id=0, has_side_effects=True),
        name="exchange",
    )(*[in_hbm(x) for x in (
        coarse_children.T, fine_neighbours.T, coarse_feat, up_weight, up_bias[None, :], conv_weight, conv_bias[None, :])])
    return pl.pallas_call(
        main_kernel,
        out_shape=jax.ShapeDtypeStruct((OWN, 32, 512), BF16),
        in_specs=[SMEM] + [VMEM] * 6,
        out_specs=ANY,
        scratch_shapes=[
            pltpu.VMEM((ACTIVE, 16, 1280), BF16),
            pltpu.VMEM((2, SLOTS + 1, 64, 128), F32),
            pltpu.VMEM((GROUP, 64, CONV_K), BF16),
            pltpu.VMEM((GROUP, 64, CONV_K), BF16),
            pltpu.VMEM((OWN, 32, 512), BF16),
            pltpu.SemaphoreType.DMA((3,)),
            pltpu.SemaphoreType.DMA((2,)),
        ],
        compiler_params=pltpu.CompilerParams(vmem_limit_bytes=28 * 2 ** 20),
        name="convolutions",
    )(near, octs, up_w, conv_w, bias, inner_hidden, inner_out)


def solution(mesh):
    in_specs = (
        P(AXES, None, None),
        P(AXES, None),
        P(AXES, None),
        P(),
        P(),
        P(),
        P(),
    )
    return jax.shard_map(
        on_device, mesh=mesh, in_specs=in_specs, out_specs=P(AXES, None, None), check_vma=False
    )
```

```python
import jax
import jax.numpy as jnp
from jax import lax
from jax.experimental import pallas as pl
from jax.experimental.pallas import tpu as pltpu
from jax.sharding import PartitionSpec as P

F32 = jnp.float32
BF16 = jnp.bfloat16
AXES = ("row", "col")
HALO = 12
OWN = 48
SLOTS = OWN + 3 * HALO
ACTIVE = OWN + 2 * HALO
REACH = 3 * OWN
PACK = 6
SPREAD = 6
GROUP = 6
INNER = OWN - HALO
EXTRA_AT = 9 * 256
CONV_K = EXTRA_AT + 5 * 128

direction_list = [
    (code // 9 - 1, code // 3 % 3 - 1, code % 3 - 1) for code in range(27) if code != 13
]
column_of = {delta: column for column, delta in enumerate(direction_list)}
upward_list = [(0, 0, 1), (0, 1, 0), (0, 1, 1), (1, 0, 0), (1, 0, 1), (1, 1, 0), (1, 1, 1)]
upward_columns = [column_of[delta] for delta in upward_list]

CLASSES = [
    ((0, 0), 256, 512, {(0, 0): (1, 1)}),
    ((0, 1), 256, 768, {(0, 0): (1, 2), (0, 1): (1, 0)}),
    ((1, 0), 0, 512, {(0, 0): (2, 1), (1, 0): (0, 1)}),
    ((1, 1), 0, 1024, {(0, 0): (2, 2), (0, 1): (2, 0), (1, 0): (0, 2), (1, 1): (0, 0)}),
]
SHIFT_AT = {(1, 0): 0, (0, 0): 256, (0, 1): 512, (1, 1): 768}
HALO_AT = 1024
class_starts = []
UP_MAIN = 0
for _, low, high, _ in CLASSES:
    class_starts.append(UP_MAIN)
    UP_MAIN += high - low
UP_K = UP_MAIN + 256


def iota(shape, dim):
    return lax.broadcasted_iota(jnp.int32, shape, dim)


def exchange_kernel(children_hbm, near_hbm, feat_hbm, up_hbm, up_b_hbm, conv_hbm, conv_b_hbm,
                    octs_ref, near_out, up_out, conv_out, bias_out, inner_hidden, inner_out,
                    children_ref, near_v, feat_ref, up_ref, up_b, conv_ref, conv_b,
                    table, slots, source_v, source, from_next, from_prev, low_own, edge_own, high_own, halo_next, edge_next, halo_prev,
                    near_pad, near_next, near_prev, inner_near_v, inner_near, shifted, patches_0, patches_1,
                    send_sem, recv_sem, fetch_sem, feat_sem):
    columns = lax.axis_size("col")
    ranks = lax.axis_size("row") * columns
    rank = lax.axis_index("row") * columns + lax.axis_index("col")
    exists = {-1: rank > 0, 1: rank < ranks - 1}

    def device(offset):
        other = lax.rem(rank + offset + ranks, ranks)
        return other // columns, lax.rem(other, columns)

    barrier = pltpu.get_barrier_semaphore()
    for offset in (1, -1):
        @pl.when(exists[offset])
        def _(offset=offset):
            pl.semaphore_signal(barrier, inc=1, device_id=device(offset), device_id_type=pl.DeviceIdType.MESH)

    fetches = [pltpu.make_async_copy(src, dst, fetch_sem.at[number]) for number, (src, dst) in enumerate((
        (children_hbm, children_ref), (near_hbm, near_v), (up_hbm, up_ref), (conv_hbm, conv_ref),
        (up_b_hbm, up_b), (conv_b_hbm, conv_b)))]

    def feat_fetch(step):
        part = pl.ds(step * PACK, PACK)
        return pltpu.make_async_copy(feat_hbm.at[part], feat_ref.at[part], feat_sem.at[step])

    fetches[0].start()
    for step in range(12 // PACK):
        feat_fetch(step).start()
    for fetch in fetches[1:]:
        fetch.start()

    fetches[0].wait()
    slot_id = iota((8, 128), 0) * 128 + iota((8, 128), 1)
    first = (rank - 1) * OWN
    chosen = jnp.full((8, 128), 96, jnp.int32)
    for c in range(12):
        for o in range(8):
            child = children_ref[o, c]
            position = jnp.where(child >= 0, child - first, REACH)
            chosen = jnp.where(slot_id == position, 8 * c + o, chosen)
    source_v[...] = chosen
    source_copy = pltpu.make_async_copy(source_v, source, fetch_sem.at[6])
    source_copy.start()

    low_lane = iota((64, 128), 1) < 64
    low_row = iota((8, 128), 0) < 4
    table[96] = jnp.zeros((16, 256), BF16)

    def turn(c, pair):
        near = feat_ref[c, :, 128 * pair:128 * pair + 128].astype(F32)
        far = feat_ref[c, :, 256 + 128 * pair:384 + 128 * pair].astype(F32)
        top = jnp.where(low_lane, near, pltpu.roll(far, 64, 1))
        bottom = jnp.where(low_lane, pltpu.roll(near, 64, 1), far)
        return jnp.concatenate([top, bottom], axis=0).T

    def octants_of(turned):
        listed = []
        for octant in range(8):
            ox, oy, oz = octant // 4, octant // 2 % 2, octant % 2
            sheets = []
            for y in range(4):
                at = 64 * ox + 8 * (4 * oy + y)
                sheets.append(turned[at:at + 8])
            halves = []
            for one, two in ((sheets[0], sheets[1]), (sheets[2], sheets[3])):
                if oz == 0:
                    halves.append(jnp.where(low_row, one, pltpu.roll(two, 4, 0)))
                else:
                    halves.append(jnp.where(low_row, pltpu.roll(one, 4, 0), two))
            listed.append(jnp.concatenate(halves, axis=0).astype(BF16))
        return listed

    def coarse_blocks(step, _):
        feat_fetch(step).wait()
        turned = [[turn(step * PACK + k, pair) for pair in range(2)] for k in range(PACK)]
        for k in range(PACK):
            for pair in range(2):
                for octant, value in enumerate(octants_of(turned[k][pair])):
                    table[(step * PACK + k) * 8 + octant, :, 128 * pair:128 * pair + 128] = value
        return 0

    lax.fori_loop(0, 12 // PACK, coarse_blocks, 0)
    source_copy.wait()
    fetches[1].wait()
    near_pad[...] = jnp.zeros((32, 128), jnp.int32)
    near_pad[0:26, 0:48] = near_v[...]
    inside = near_pad[...] - rank * OWN
    within = (near_pad[...] >= 0) & (inside >= 0) & (inside < OWN)
    inner_near_v[0:32] = jnp.where(within, inside + HALO, SLOTS)
    inner_near_v[32:64] = jnp.where(within & (inside < INNER), inside, INNER)
    inner_copy = pltpu.make_async_copy(inner_near_v, inner_near, fetch_sem.at[7])
    inner_copy.start()

    def octant_at(q):
        return table[source[q // 128, q % 128]]

    def fill(start, q_start):
        def body(k, _):
            for j in range(8):
                slots[start + k * 8 + j] = octant_at(q_start + k * 8 + j)
            return 0
        lax.fori_loop(0, OWN // 16, body, 0)

    half = OWN // 2
    plan = [
        (slots.at[0:half], from_next.at[0:half], -1),
        (slots.at[OWN:OWN + half], from_prev.at[0:half], 1),
        (slots.at[half:OWN], from_next.at[half:OWN], -1),
        (slots.at[OWN + half:2 * OWN], from_prev.at[half:OWN], 1),
        (near_pad, near_next, -1),
        (near_pad, near_prev, 1),
        (low_own, halo_next, -1),
        (high_own, halo_prev, 1),
        (edge_own, edge_next, -1),
    ]

    def transfer(number):
        src, dst, offset = plan[number]
        return pltpu.make_async_remote_copy(
            src_ref=src, dst_ref=dst, send_sem=send_sem.at[number], recv_sem=recv_sem.at[number],
            device_id=device(offset), device_id_type=pl.DeviceIdType.MESH)

    def send(*numbers):
        for number in numbers:
            @pl.when(exists[plan[number][2]])
            def _(number=number):
                transfer(number).start()

    def sent(*numbers):
        for number in numbers:
            @pl.when(exists[plan[number][2]])
            def _(number=number):
                transfer(number).wait_send()

    def landed(*numbers):
        for number in numbers:
            @pl.when(exists[-plan[number][2]])
            def _(number=number):
                transfer(number).wait_recv()

    for offset, refs, near in ((1, (from_next, halo_next, edge_next), near_next), (-1, (from_prev, halo_prev), near_prev)):
        @pl.when(jnp.logical_not(exists[offset]))
        def _(refs=refs, near=near):
            for ref in refs:
                ref[...] = jnp.zeros(ref.shape, BF16)
            near[...] = jnp.full((32, 128), -1, jnp.int32)

    fill(0, 0)
    fill(OWN, 2 * OWN)
    pl.semaphore_wait(barrier, exists[1].astype(jnp.int32) + exists[-1].astype(jnp.int32))
    send(0, 1)
    fill(half, half)
    fill(OWN + half, 2 * OWN + half)
    send(2, 3, 4, 5)

    for fetch in fetches[2:]:
        fetch.wait()
    make_weights(up_ref, conv_ref, up_out, conv_out)
    spread = (iota((32, 256), 0) == iota((32, 256), 1) % 32).astype(F32)
    for number, ref in enumerate((up_b, conv_b)):
        bias_out[8 * number:8 * number + 8] = jnp.dot(
            jnp.broadcast_to(ref[...], (8, 32)), spread, precision=lax.Precision.HIGHEST,
            preferred_element_type=F32)
    octs_ref[SLOTS] = jnp.zeros((16, 256), F32)
    inner_hidden[:, INNER] = jnp.zeros((2, 64, 128), F32)
    inner_copy.wait()

    def join(start, stop, copy_ref, offset):
        def body(k, _):
            for j in range(4):
                b = start + k * 4 + j
                total = octant_at(OWN + b).astype(F32) + from_next[b].astype(F32) + from_prev[b].astype(F32)
                octs_ref[HALO + b] = total
                if copy_ref is not None:
                    copy_ref[b - offset] = total.astype(BF16)
            return 0
        lax.fori_loop(0, (stop - start) // 4, body, 0)

    sub = iota((8, 128), 0)

    def join_low(k, _):
        for j in range(2):
            edges = []
            for b in (k * 4 + 2 * j, k * 4 + 2 * j + 1):
                total = octant_at(OWN + b).astype(F32) + from_next[b].astype(F32) + from_prev[b].astype(F32)
                octs_ref[HALO + b] = total
                low_own[b] = total[:, 0:128].astype(BF16)
                first, second = total[0:8, 128:256], total[8:16, 128:256]
                edges.append(jnp.where(sub < 5, first, jnp.where(
                    sub == 5, pltpu.roll(second, 5, 0), pltpu.roll(second, 2, 0))))
            edge_own[k * 2 + j] = jnp.concatenate(edges, axis=0).astype(BF16)
        return 0

    landed(0, 1)
    lax.fori_loop(0, half // 4, join_low, 0)
    send(6, 8)
    landed(2, 3)
    join(OWN - HALO, OWN, high_own, OWN - HALO)
    send(7)
    join(half, OWN - HALO, None, 0)

    spread_octants(inner_near, octs_ref, shifted, HALO, 0, INNER)
    up_bias = bias_out[0:1]

    def inner_upsample(chunk, _):
        upsample(shifted, up_out, up_bias, inner_hidden, chunk * (INNER // 2), INNER // 2)
        return 0

    lax.fori_loop(0, 2, inner_upsample, 0)
    build_group, convolve = convolver(
        lambda column, b: inner_near[32 + column, b], 0, inner_hidden, conv_out, bias_out[8:9], inner_out, HALO)
    build_group(patches_0, HALO)
    build_group(patches_1, HALO + GROUP)
    convolve(patches_0, HALO)
    convolve(patches_1, HALO + GROUP)
    landed(4, 5)
    lane = iota((32, 128), 1)
    near = jnp.where(lane < HALO, pltpu.roll(near_prev[...], 128 - (OWN - HALO), 1),
                     jnp.where(lane < HALO + OWN, pltpu.roll(near_pad[...], HALO, 1),
                               pltpu.roll(near_next[...], HALO + OWN, 1)))
    moved = near - (rank * OWN - HALO)
    near_out[...] = jnp.where((near >= 0) & (moved >= 0) & (moved < SLOTS), moved, SLOTS)
    landed(7)
    octs_ref[0:HALO] = halo_prev[...].astype(F32)
    landed(6, 8)

    def spread_low(k, _):
        edges = edge_next[k].astype(F32)
        for j in range(2):
            u = HALO + OWN + 2 * k + j
            octs_ref[u, :, 0:128] = halo_next[2 * k + j].astype(F32)
            edge = edges[8 * j:8 * j + 8]
            octs_ref[u, 0:8, 128:256] = edge
            octs_ref[u, 8:16, 128:256] = jnp.where(sub == 0, pltpu.roll(edge, 3, 0), pltpu.roll(edge, 6, 0))
        return 0

    lax.fori_loop(0, HALO, spread_low, 0)
    sent(*range(9))


def make_weights(up_ref, conv_ref, up_out, conv_out):
    spread = (iota((32, 256), 0) == iota((32, 256), 1) % 32).astype(BF16)
    lane_x = iota((32, 256), 1) // 32
    zero = jnp.zeros((32, 256), F32)
    wide = lax.dot_general(conv_ref[...], spread, (((0,), (0,)), ((), ())), preferred_element_type=F32)

    def tap_of(kx, ky, kz):
        at = 32 * (9 * kx + 3 * ky + kz)
        return wide[at:at + 32]

    for ky in range(3):
        for kz in range(3):
            taps = [tap_of(kx, ky, kz) for kx in range(3)]
            for x in range(8):
                value = zero
                for kx in range(3):
                    value = jnp.where(lane_x == x + 1 - kx, taps[kx], value)
                at = 256 * (3 * ky + kz) + 32 * x
                conv_out[at:at + 32] = value.astype(BF16)
    pairs = [((0, 0), (0, 1)), ((1, 0), (1, 1)), ((2, 0), (2, 1)), ((0, 2), (1, 2)), ((2, 2), None)]
    for tile, (even, odd) in enumerate(pairs):
        at = EXTRA_AT + 128 * tile

        def beyond(tap):
            return zero if tap is None else jnp.where(lane_x == 7, tap_of(2, *tap), zero)

        def before(tap):
            return zero if tap is None else jnp.where(lane_x == 0, tap_of(0, *tap), zero)

        conv_out[at:at + 32] = beyond(even).astype(BF16)
        conv_out[at + 32:at + 64] = before(odd).astype(BF16)
        conv_out[at + 64:at + 96] = beyond(odd).astype(BF16)
        conv_out[at + 96:at + 128] = before(even).astype(BF16)

    lane_f = iota((64, 256), 1) // 32
    zero_up = jnp.zeros((64, 256), F32)

    def up_tap(kx, ky, kz):
        code = 9 * kx + 3 * ky + kz
        return jnp.dot(up_ref[:, 32 * code:32 * code + 32], spread, preferred_element_type=F32)

    for (_, low, high, taps_of), start in zip(CLASSES, class_starts):
        for shift, at_lane in SHIFT_AT.items():
            if not low <= at_lane < high:
                continue
            at = start + at_lane - low
            taps = [up_tap(kx, *taps_of[shift]) for kx in range(3)]
            for x in range(4):
                value = zero_up
                for kx in range(3):
                    value = jnp.where(lane_f == 2 * x + kx - 1, taps[kx], value)
                up_out[at + 64 * x:at + 64 * x + 64] = value.astype(BF16)
    for number, shift in enumerate(((0, 0), (0, 1), (1, 0), (1, 1))):
        value = zero_up
        for k, (_, _, _, taps_of) in enumerate(CLASSES):
            if shift in taps_of:
                group = 4 * (k % 2) + (3 if k < 2 else 2)
                value = jnp.where(lane_f == group, up_tap(0, *taps_of[shift]), value)
        at = UP_MAIN + 64 * number
        up_out[at:at + 64] = value.astype(BF16)


def spread_octants(near_ref, octs, shifted, offset, start, stop):
    def shift_z(value, beyond):
        last = iota(value.shape, 0) % 4 == 3
        return jnp.where(last, pltpu.roll(beyond, 3, 0), pltpu.roll(value, 15, 0))

    def shift_y(value, beyond):
        first = iota(value.shape, 0) < 4
        return pltpu.roll(jnp.where(first, beyond, value), 12, 0)

    low_lane16 = iota((16, 128), 1) < 64

    def spread_octant(h):
        at = [near_ref[column, h] for column in upward_columns]
        here, z_next, y_next, yz_next = octs[h + offset], octs[at[0]], octs[at[1]], octs[at[2]]
        by_z = shift_z(here, z_next)
        x0, xz, xy, xyz = [octs[at[j], :, 0:128] for j in (3, 4, 5, 6)]
        x_by_z = shift_z(x0, xz)
        x_by_y = shift_y(x0, xy)
        x_by_yz = shift_y(x_by_z, shift_z(xy, xyz))
        return [
            (0, shift_y(here, y_next)),
            (256, here),
            (512, by_z),
            (768, shift_y(by_z, shift_z(y_next, yz_next))),
            (1024, jnp.where(low_lane16, x0, pltpu.roll(x_by_z, 64, 1))),
            (1152, jnp.where(low_lane16, x_by_y, pltpu.roll(x_by_yz, 64, 1))),
        ]

    def group_of(group, _):
        for h, parts in [(group * SPREAD + k, spread_octant(group * SPREAD + k)) for k in range(SPREAD)]:
            for lane, value in parts:
                shifted[h, :, lane:lane + value.shape[1]] = value.astype(BF16)
        return 0

    lax.fori_loop(start // SPREAD, stop // SPREAD, group_of, 0)


def upsample(shifted, up_w, up_bias, hidden, start, count):
    def product(low, high, at):
        rows = shifted[pl.ds(start, count), :, low:high].reshape(16 * count, high - low)
        return jnp.dot(rows, up_w[at:at + high - low], preferred_element_type=F32)

    halo = product(HALO_AT, HALO_AT + 256, UP_MAIN)
    reached = iota((16 * count, 128), 1) >= 96
    for k, (((py, pz), low, high, _), at) in enumerate(zip(CLASSES, class_starts)):
        beyond = halo[:, 128 * (k % 2):128 * (k % 2) + 128]
        if k >= 2:
            beyond = pltpu.roll(beyond, 32, 1)
        value = product(low, high, at) + up_bias
        tiles = [value[:, 0:128], value[:, 128:256] + jnp.where(reached, beyond, 0.0)]
        for tile in range(2):
            half = 0.5 * tiles[tile]
            value = half + half * jnp.tanh(half)
            for b in range(count):
                for y in range(4):
                    hidden[tile, start + b, pl.ds(8 * (2 * y + py) + pz, 4, stride=2), :] = (
                        value[16 * b + 4 * y:16 * b + 4 * y + 4])


def convolver(nearby, offset, hidden, conv_w, conv_bias, out_ref, out_offset):
    row = iota((8, 128), 0)
    first_row, last_row = row == 0, row == 7
    low_lane8 = iota((8, 128), 1) < 64
    lane = iota((8, 128), 1)
    even_lane = (lane < 32) | (lane >= 96)
    low_lane32 = iota((32, 128), 1) < 64

    def shift_row(dz, value, beyond):
        if dz == 0:
            return value
        if dz == 1:
            return pltpu.roll(jnp.where(first_row, beyond, value), 7, 0)
        return pltpu.roll(jnp.where(last_row, beyond, value), 1, 0)

    def two(one, other):
        return jnp.concatenate([one, other], axis=0).astype(BF16)

    def build(patches, b, k):
        at = {delta: nearby(column, b) for delta, column in column_of.items()}
        at[(0, 0, 0)] = b + offset

        def sheet(delta, y, tile):
            return hidden[tile, at[delta], 8 * y:8 * y + 8, :]

        def side(dy, dz, y):
            return jnp.where(low_lane8, sheet((1, dy, dz), y, 0), sheet((-1, dy, dz), y, 1))

        def sheets(dz, take):
            listed = []
            for step in range(10):
                dy = -1 if step == 0 else (1 if step == 9 else 0)
                y = (step - 1) % 8
                beyond = None if dz == 0 else take(dy, dz, y)
                listed.append(shift_row(dz, take(dy, 0, y), beyond))
            return listed

        def put(values, ky, at_lane):
            for pair in range(4):
                patches[k, 16 * pair:16 * pair + 16, at_lane:at_lane + 128] = values[pair]

        def put_all(listed, lanes):
            even = [two(listed[2 * n], listed[2 * n + 1]) for n in range(5)]
            odd = [two(listed[2 * n + 1], listed[2 * n + 2]) for n in range(4)]
            put(even[0:4], 0, lanes[0])
            put(odd, 1, lanes[1])
            put(even[1:5], 2, lanes[2])

        for dz in (-1, 0, 1):
            for tile in range(2):
                listed = sheets(dz, lambda dy, dz_, y: sheet((0, dy, dz_), y, tile))
                put_all(listed, [256 * (3 * ky + dz + 1) + 128 * tile for ky in range(3)])
        sides = [sheets(dz, side) for dz in (-1, 0, 1)]
        joined = [jnp.where(even_lane, one, pltpu.roll(other, 64, 1)) for one, other in zip(sides[0], sides[1])]
        put_all(joined, [EXTRA_AT + 128 * ky for ky in range(3)])
        last = sides[2]
        paired = [jnp.where(even_lane, last[n], pltpu.roll(last[n + 1], 64, 1)) for n in range(8)]
        put([two(paired[2 * n], paired[2 * n + 1]) for n in range(4)], 0, EXTRA_AT + 384)
        put([two(last[2 * n + 2], last[2 * n + 3]) for n in range(4)], 0, EXTRA_AT + 512)

    def convolve(patches, base):
        value = jnp.dot(patches[...].reshape(64 * GROUP, CONV_K), conv_w[...], preferred_element_type=F32) + conv_bias
        for pair in range(GROUP // 2):
            for half in range(2):
                turned = value[128 * pair:128 * pair + 128, 128 * half:128 * half + 128].T
                for x in range(0, 4, 2):
                    one, other = turned[32 * x:32 * x + 32], turned[32 * x + 32:32 * x + 64]
                    at = 256 * half + 64 * x
                    b = base + 2 * pair
                    out_ref[b - out_offset, :, at:at + 128] = jnp.where(
                        low_lane32, one, pltpu.roll(other, 64, 1)).astype(BF16)
                    out_ref[b + 1 - out_offset, :, at:at + 128] = jnp.where(
                        low_lane32, pltpu.roll(one, 64, 1), other).astype(BF16)

    def build_group(patches, base):
        for k in range(GROUP):
            build(patches, base + k, k)

    return build_group, convolve


def main_kernel(near_ref, octs, up_w, conv_w, bias, inner_hidden, inner_out, out_hbm,
                shifted, hidden, patches_0, patches_1, out_ref, out_sem, inner_sem):
    bring = pltpu.make_async_copy(inner_hidden.at[:, 0:INNER], hidden.at[:, HALO:HALO + INNER], inner_sem.at[0])
    bring.start()
    middle = pltpu.make_async_copy(inner_out, out_hbm.at[HALO:2 * HALO], inner_sem.at[1])
    middle.start()
    hidden[:, SLOTS] = jnp.zeros((2, 64, 128), F32)
    spread_octants(near_ref, octs, shifted, 0, 0, HALO)
    spread_octants(near_ref, octs, shifted, 0, HALO + INNER, ACTIVE)
    up_bias = bias[0:1]
    upsample(shifted, up_w, up_bias, hidden, 0, HALO)
    upsample(shifted, up_w, up_bias, hidden, HALO + INNER, 2 * HALO)
    bring.wait()

    build_group, convolve = convolver(
        lambda column, b: near_ref[column, b + HALO], HALO, hidden, conv_w, bias[8:9], out_ref, 0)

    def base_of(step):
        return jnp.where(step > 0, 2 * GROUP * (step + 1), 0)

    def write_out(step):
        part = pl.ds(base_of(step), 2 * GROUP)
        return pltpu.make_async_copy(out_ref.at[part], out_hbm.at[part], out_sem.at[step])

    build_group(patches_0, 0)

    def groups(step, _):
        base = base_of(step)
        build_group(patches_1, base + GROUP)
        convolve(patches_0, base)
        build_group(patches_0, base_of(jnp.minimum(step + 1, 2)))
        convolve(patches_1, base + GROUP)
        write_out(step).start()
        return 0

    lax.fori_loop(0, 3, groups, 0)
    middle.wait()
    for step in range(3):
        write_out(step).wait()


VMEM = pl.BlockSpec(memory_space=pltpu.VMEM)
SMEM = pl.BlockSpec(memory_space=pltpu.SMEM)
ANY = pl.BlockSpec(memory_space=pltpu.MemorySpace.HBM)


def in_hbm(array):
    return pltpu.with_memory_space_constraint(array, pltpu.HBM)


def on_device(
    coarse_feat, coarse_children, fine_neighbours, up_weight, up_bias, conv_weight, conv_bias
):
    octs, near, up_w, conv_w, bias, inner_hidden, inner_out = pl.pallas_call(
        exchange_kernel,
        out_shape=[
            jax.ShapeDtypeStruct((SLOTS + 1, 16, 256), F32),
            jax.ShapeDtypeStruct((32, 128), jnp.int32),
            jax.ShapeDtypeStruct((UP_K, 256), BF16),
            jax.ShapeDtypeStruct((CONV_K, 256), BF16),
            jax.ShapeDtypeStruct((16, 256), F32),
            jax.ShapeDtypeStruct((2, INNER + 1, 64, 128), F32),
            jax.ShapeDtypeStruct((HALO, 32, 512), BF16),
        ],
        in_specs=[ANY] * 7,
        out_specs=[VMEM] * 7,
        scratch_shapes=[
            pltpu.SMEM((8, 12), jnp.int32),
            pltpu.VMEM((26, OWN), jnp.int32),
            pltpu.VMEM((12, 64, 512), BF16),
            pltpu.VMEM((64, 864), BF16),
            pltpu.VMEM((1, 32), F32),
            pltpu.VMEM((32, 864), BF16),
            pltpu.VMEM((1, 32), F32),
            pltpu.VMEM((97, 16, 256), BF16),
            pltpu.VMEM((2 * OWN, 16, 256), BF16),
            pltpu.VMEM((8, 128), jnp.int32),
            pltpu.SMEM((8, 128), jnp.int32),
            pltpu.VMEM((OWN, 16, 256), BF16),
            pltpu.VMEM((OWN, 16, 256), BF16),
            pltpu.VMEM((2 * HALO, 16, 128), BF16),
            pltpu.VMEM((HALO, 16, 128), BF16),
            pltpu.VMEM((HALO, 16, 256), BF16),
            pltpu.VMEM((2 * HALO, 16, 128), BF16),
            pltpu.VMEM((HALO, 16, 128), BF16),
            pltpu.VMEM((HALO, 16, 256), BF16),
            pltpu.VMEM((32, 128), jnp.int32),
            pltpu.VMEM((32, 128), jnp.int32),
            pltpu.VMEM((32, 128), jnp.int32),
            pltpu.VMEM((64, 128), jnp.int32),
            pltpu.SMEM((64, 128), jnp.int32),
            pltpu.VMEM((INNER, 16, 1280), BF16),
            pltpu.VMEM((GROUP, 64, CONV_K), BF16),
            pltpu.VMEM((GROUP, 64, CONV_K), BF16),
            pltpu.SemaphoreType.DMA((9,)),
            pltpu.SemaphoreType.DMA((9,)),
            pltpu.SemaphoreType.DMA((8,)),
            pltpu.SemaphoreType.DMA((12 // PACK,)),
        ],
        compiler_params=pltpu.CompilerParams(
            vmem_limit_bytes=32 * 2 ** 20, collective_id=0, has_side_effects=True),
        name="exchange",
    )(*[in_hbm(x) for x in (
        coarse_children.T, fine_neighbours.T, coarse_feat, up_weight, up_bias[None, :], conv_weight, conv_bias[None, :])])
    return pl.pallas_call(
        main_kernel,
        out_shape=jax.ShapeDtypeStruct((OWN, 32, 512), BF16),
        in_specs=[SMEM] + [VMEM] * 6,
        out_specs=ANY,
        scratch_shapes=[
            pltpu.VMEM((ACTIVE, 16, 1280), BF16),
            pltpu.VMEM((2, SLOTS + 1, 64, 128), F32),
            pltpu.VMEM((GROUP, 64, CONV_K), BF16),
            pltpu.VMEM((GROUP, 64, CONV_K), BF16),
            pltpu.VMEM((OWN, 32, 512), BF16),
            pltpu.SemaphoreType.DMA((3,)),
            pltpu.SemaphoreType.DMA((2,)),
        ],
        compiler_params=pltpu.CompilerParams(vmem_limit_bytes=28 * 2 ** 20),
        name="convolutions",
    )(near, octs, up_w, conv_w, bias, inner_hidden, inner_out)


def solution(mesh):
    in_specs = (
        P(AXES, None, None),
        P(AXES, None),
        P(AXES, None),
        P(),
        P(),
        P(),
        P(),
    )
    return jax.shard_map(
        on_device, mesh=mesh, in_specs=in_specs, out_specs=P(AXES, None, None), check_vma=False
    )
```

```python
import jax
import jax.numpy as jnp
from jax import lax
from jax.experimental import pallas as pl
from jax.experimental.pallas import tpu as pltpu
from jax.sharding import PartitionSpec as P

F32 = jnp.float32
BF16 = jnp.bfloat16
AXES = ("row", "col")
HALO = 12
OWN = 48
SLOTS = OWN + 3 * HALO
ACTIVE = OWN + 2 * HALO
REACH = 3 * OWN
PACK = 6
SPREAD = 6
GROUP = 6
INNER = OWN - HALO
EXTRA_AT = 9 * 256
CONV_K = EXTRA_AT + 5 * 128

direction_list = [
    (code // 9 - 1, code // 3 % 3 - 1, code % 3 - 1) for code in range(27) if code != 13
]
column_of = {delta: column for column, delta in enumerate(direction_list)}
upward_list = [(0, 0, 1), (0, 1, 0), (0, 1, 1), (1, 0, 0), (1, 0, 1), (1, 1, 0), (1, 1, 1)]
upward_columns = [column_of[delta] for delta in upward_list]

CLASSES = [
    ((0, 0), 256, 512, {(0, 0): (1, 1)}),
    ((0, 1), 256, 768, {(0, 0): (1, 2), (0, 1): (1, 0)}),
    ((1, 0), 0, 512, {(0, 0): (2, 1), (1, 0): (0, 1)}),
    ((1, 1), 0, 1024, {(0, 0): (2, 2), (0, 1): (2, 0), (1, 0): (0, 2), (1, 1): (0, 0)}),
]
SHIFT_AT = {(1, 0): 0, (0, 0): 256, (0, 1): 512, (1, 1): 768}
HALO_AT = 1024
class_starts = []
UP_MAIN = 0
for _, low, high, _ in CLASSES:
    class_starts.append(UP_MAIN)
    UP_MAIN += high - low
UP_K = UP_MAIN + 256


def iota(shape, dim):
    return lax.broadcasted_iota(jnp.int32, shape, dim)


def exchange_kernel(children_hbm, near_hbm, feat_hbm, up_hbm, up_b_hbm, conv_hbm, conv_b_hbm,
                    octs_ref, near_out, up_out, conv_out, bias_out, inner_hidden, inner_out,
                    children_ref, near_v, feat_ref, up_ref, up_b, conv_ref, conv_b,
                    table, slots, source_v, source, from_next, from_prev, low_own, edge_own, high_own, halo_next, edge_next, halo_prev,
                    near_pad, near_next, near_prev, inner_near_v, inner_near, all_near, shifted, patches_0, patches_1,
                    send_sem, recv_sem, fetch_sem, feat_sem):
    columns = lax.axis_size("col")
    ranks = lax.axis_size("row") * columns
    rank = lax.axis_index("row") * columns + lax.axis_index("col")
    exists = {-1: rank > 0, 1: rank < ranks - 1}

    def device(offset):
        other = lax.rem(rank + offset + ranks, ranks)
        return other // columns, lax.rem(other, columns)

    barrier = pltpu.get_barrier_semaphore()
    for offset in (1, -1):
        @pl.when(exists[offset])
        def _(offset=offset):
            pl.semaphore_signal(barrier, inc=1, device_id=device(offset), device_id_type=pl.DeviceIdType.MESH)

    fetches = [pltpu.make_async_copy(src, dst, fetch_sem.at[number]) for number, (src, dst) in enumerate((
        (children_hbm, children_ref), (near_hbm, near_v), (up_hbm, up_ref), (conv_hbm, conv_ref),
        (up_b_hbm, up_b), (conv_b_hbm, conv_b)))]

    def feat_fetch(step):
        part = pl.ds(step * PACK, PACK)
        return pltpu.make_async_copy(feat_hbm.at[part], feat_ref.at[part], feat_sem.at[step])

    fetches[0].start()
    for step in range(12 // PACK):
        feat_fetch(step).start()
    for fetch in fetches[1:]:
        fetch.start()

    fetches[0].wait()
    slot_id = iota((8, 128), 0) * 128 + iota((8, 128), 1)
    first = (rank - 1) * OWN
    chosen = jnp.full((8, 128), 96, jnp.int32)
    for c in range(12):
        for o in range(8):
            child = children_ref[o, c]
            position = jnp.where(child >= 0, child - first, REACH)
            chosen = jnp.where(slot_id == position, 8 * c + o, chosen)
    source_v[...] = chosen
    source_copy = pltpu.make_async_copy(source_v, source, fetch_sem.at[6])
    source_copy.start()

    low_lane = iota((64, 128), 1) < 64
    low_row = iota((8, 128), 0) < 4
    table[96] = jnp.zeros((16, 256), BF16)

    def turn(c, pair):
        near = feat_ref[c, :, 128 * pair:128 * pair + 128].astype(F32)
        far = feat_ref[c, :, 256 + 128 * pair:384 + 128 * pair].astype(F32)
        top = jnp.where(low_lane, near, pltpu.roll(far, 64, 1))
        bottom = jnp.where(low_lane, pltpu.roll(near, 64, 1), far)
        return jnp.concatenate([top, bottom], axis=0).T

    def octants_of(turned):
        listed = []
        for octant in range(8):
            ox, oy, oz = octant // 4, octant // 2 % 2, octant % 2
            sheets = []
            for y in range(4):
                at = 64 * ox + 8 * (4 * oy + y)
                sheets.append(turned[at:at + 8])
            halves = []
            for one, two in ((sheets[0], sheets[1]), (sheets[2], sheets[3])):
                if oz == 0:
                    halves.append(jnp.where(low_row, one, pltpu.roll(two, 4, 0)))
                else:
                    halves.append(jnp.where(low_row, pltpu.roll(one, 4, 0), two))
            listed.append(jnp.concatenate(halves, axis=0).astype(BF16))
        return listed

    def coarse_blocks(step, _):
        feat_fetch(step).wait()
        turned = [[turn(step * PACK + k, pair) for pair in range(2)] for k in range(PACK)]
        for k in range(PACK):
            for pair in range(2):
                for octant, value in enumerate(octants_of(turned[k][pair])):
                    table[(step * PACK + k) * 8 + octant, :, 128 * pair:128 * pair + 128] = value
        return 0

    lax.fori_loop(0, 12 // PACK, coarse_blocks, 0)
    source_copy.wait()
    fetches[1].wait()
    near_pad[...] = jnp.zeros((32, 128), jnp.int32)
    near_pad[0:26, 0:48] = near_v[...]
    inside = near_pad[...] - rank * OWN
    within = (near_pad[...] >= 0) & (inside >= 0) & (inside < OWN + HALO)
    inner_near_v[0:32] = jnp.where(within, inside + HALO, SLOTS)
    inner_near_v[32:64] = jnp.where(within, inside + HALO, ACTIVE)
    inner_copy = pltpu.make_async_copy(inner_near_v, inner_near, fetch_sem.at[7])
    inner_copy.start()

    def octant_at(q):
        return table[source[q // 128, q % 128]]

    def fill(start, q_start):
        def body(k, _):
            for j in range(8):
                slots[start + k * 8 + j] = octant_at(q_start + k * 8 + j)
            return 0
        lax.fori_loop(0, OWN // 16, body, 0)

    half = OWN // 2
    plan = [
        (slots.at[0:half], from_next.at[0:half], -1),
        (slots.at[OWN:OWN + half], from_prev.at[0:half], 1),
        (slots.at[half:OWN], from_next.at[half:OWN], -1),
        (slots.at[OWN + half:2 * OWN], from_prev.at[half:OWN], 1),
        (near_pad, near_next, -1),
        (near_pad, near_prev, 1),
        (low_own, halo_next, -1),
        (high_own, halo_prev, 1),
        (edge_own, edge_next, -1),
    ]

    def transfer(number):
        src, dst, offset = plan[number]
        return pltpu.make_async_remote_copy(
            src_ref=src, dst_ref=dst, send_sem=send_sem.at[number], recv_sem=recv_sem.at[number],
            device_id=device(offset), device_id_type=pl.DeviceIdType.MESH)

    def send(*numbers):
        for number in numbers:
            @pl.when(exists[plan[number][2]])
            def _(number=number):
                transfer(number).start()

    def sent(*numbers):
        for number in numbers:
            @pl.when(exists[plan[number][2]])
            def _(number=number):
                transfer(number).wait_send()

    def landed(*numbers):
        for number in numbers:
            @pl.when(exists[-plan[number][2]])
            def _(number=number):
                transfer(number).wait_recv()

    for offset, refs, near in ((1, (from_next, halo_next, edge_next), near_next), (-1, (from_prev, halo_prev), near_prev)):
        @pl.when(jnp.logical_not(exists[offset]))
        def _(refs=refs, near=near):
            for ref in refs:
                ref[...] = jnp.zeros(ref.shape, BF16)
            near[...] = jnp.full((32, 128), -1, jnp.int32)

    fill(0, 0)
    fill(OWN, 2 * OWN)
    pl.semaphore_wait(barrier, exists[1].astype(jnp.int32) + exists[-1].astype(jnp.int32))
    send(0, 1)
    fill(half, half)
    fill(OWN + half, 2 * OWN + half)
    send(2, 3, 4, 5)

    for fetch in fetches[2:]:
        fetch.wait()
    make_weights(up_ref, conv_ref, up_out, conv_out)
    spread = (iota((32, 256), 0) == iota((32, 256), 1) % 32).astype(F32)
    for number, ref in enumerate((up_b, conv_b)):
        bias_out[8 * number:8 * number + 8] = jnp.dot(
            jnp.broadcast_to(ref[...], (8, 32)), spread, precision=lax.Precision.HIGHEST,
            preferred_element_type=F32)
    octs_ref[SLOTS] = jnp.zeros((16, 256), F32)
    inner_hidden[:, ACTIVE] = jnp.zeros((2, 64, 128), F32)
    inner_copy.wait()

    def join(start, stop, copy_ref, offset):
        def body(k, _):
            for j in range(4):
                b = start + k * 4 + j
                total = octant_at(OWN + b).astype(F32) + from_next[b].astype(F32) + from_prev[b].astype(F32)
                octs_ref[HALO + b] = total
                if copy_ref is not None:
                    copy_ref[b - offset] = total.astype(BF16)
            return 0
        lax.fori_loop(0, (stop - start) // 4, body, 0)

    sub = iota((8, 128), 0)

    def join_low(k, _):
        for j in range(2):
            edges = []
            for b in (k * 4 + 2 * j, k * 4 + 2 * j + 1):
                total = octant_at(OWN + b).astype(F32) + from_next[b].astype(F32) + from_prev[b].astype(F32)
                octs_ref[HALO + b] = total
                low_own[b] = total[:, 0:128].astype(BF16)
                first, second = total[0:8, 128:256], total[8:16, 128:256]
                edges.append(jnp.where(sub < 5, first, jnp.where(
                    sub == 5, pltpu.roll(second, 5, 0), pltpu.roll(second, 2, 0))))
            edge_own[k * 2 + j] = jnp.concatenate(edges, axis=0).astype(BF16)
        return 0

    landed(0, 1)
    lax.fori_loop(0, half // 4, join_low, 0)
    send(6, 8)
    landed(2, 3)
    join(OWN - HALO, OWN, high_own, OWN - HALO)
    send(7)
    join(half, OWN - HALO, None, 0)

    landed(4, 5)
    lane = iota((32, 128), 1)
    near = jnp.where(lane < HALO, pltpu.roll(near_prev[...], 128 - (OWN - HALO), 1),
                     jnp.where(lane < HALO + OWN, pltpu.roll(near_pad[...], HALO, 1),
                               pltpu.roll(near_next[...], HALO + OWN, 1)))
    moved = near - (rank * OWN - HALO)
    near_out[...] = jnp.where((near >= 0) & (moved >= 0) & (moved < SLOTS), moved, SLOTS)
    near_copy = pltpu.make_async_copy(near_out, all_near, fetch_sem.at[8])
    near_copy.start()

    spread_octants(inner_near, octs_ref, shifted, HALO, 0, INNER)
    up_bias = bias_out[0:1]

    def inner_upsample(chunk, _):
        upsample(shifted, up_out, up_bias, inner_hidden, chunk * (INNER // 2), INNER // 2, HALO)
        return 0

    lax.fori_loop(0, 2, inner_upsample, 0)
    build_group, convolve = convolver(
        lambda column, b: inner_near[32 + column, b], HALO, inner_hidden, conv_out, bias_out[8:9], inner_out, HALO)

    def middle_groups(step, _):
        base = HALO + 2 * GROUP * step
        build_group(patches_0, base)
        build_group(patches_1, base + GROUP)
        convolve(patches_0, base)
        convolve(patches_1, base + GROUP)
        return 0

    lax.fori_loop(0, 1, middle_groups, 0)

    near_copy.wait()
    landed(6, 8)

    def spread_low(k, _):
        edges = edge_next[k].astype(F32)
        for j in range(2):
            u = HALO + OWN + 2 * k + j
            octs_ref[u, :, 0:128] = halo_next[2 * k + j].astype(F32)
            edge = edges[8 * j:8 * j + 8]
            octs_ref[u, 0:8, 128:256] = edge
            octs_ref[u, 8:16, 128:256] = jnp.where(sub == 0, pltpu.roll(edge, 3, 0), pltpu.roll(edge, 6, 0))
        return 0

    lax.fori_loop(0, HALO, spread_low, 0)
    spread_octants(all_near, octs_ref, shifted, 0, HALO + INNER, ACTIVE)
    upsample(shifted, up_out, up_bias, inner_hidden, HALO + INNER, 2 * HALO)
    lax.fori_loop(1, 3, middle_groups, 0)

    landed(7)
    octs_ref[0:HALO] = halo_prev[...].astype(F32)
    sent(*range(9))


def make_weights(up_ref, conv_ref, up_out, conv_out):
    spread = (iota((32, 256), 0) == iota((32, 256), 1) % 32).astype(BF16)
    lane_x = iota((32, 256), 1) // 32
    zero = jnp.zeros((32, 256), F32)
    wide = lax.dot_general(conv_ref[...], spread, (((0,), (0,)), ((), ())), preferred_element_type=F32)

    def tap_of(kx, ky, kz):
        at = 32 * (9 * kx + 3 * ky + kz)
        return wide[at:at + 32]

    for ky in range(3):
        for kz in range(3):
            taps = [tap_of(kx, ky, kz) for kx in range(3)]
            for x in range(8):
                value = zero
                for kx in range(3):
                    value = jnp.where(lane_x == x + 1 - kx, taps[kx], value)
                at = 256 * (3 * ky + kz) + 32 * x
                conv_out[at:at + 32] = value.astype(BF16)
    pairs = [((0, 0), (0, 1)), ((1, 0), (1, 1)), ((2, 0), (2, 1)), ((0, 2), (1, 2)), ((2, 2), None)]
    for tile, (even, odd) in enumerate(pairs):
        at = EXTRA_AT + 128 * tile

        def beyond(tap):
            return zero if tap is None else jnp.where(lane_x == 7, tap_of(2, *tap), zero)

        def before(tap):
            return zero if tap is None else jnp.where(lane_x == 0, tap_of(0, *tap), zero)

        conv_out[at:at + 32] = beyond(even).astype(BF16)
        conv_out[at + 32:at + 64] = before(odd).astype(BF16)
        conv_out[at + 64:at + 96] = beyond(odd).astype(BF16)
        conv_out[at + 96:at + 128] = before(even).astype(BF16)

    lane_f = iota((64, 256), 1) // 32
    zero_up = jnp.zeros((64, 256), F32)

    def up_tap(kx, ky, kz):
        code = 9 * kx + 3 * ky + kz
        return jnp.dot(up_ref[:, 32 * code:32 * code + 32], spread, preferred_element_type=F32)

    for (_, low, high, taps_of), start in zip(CLASSES, class_starts):
        for shift, at_lane in SHIFT_AT.items():
            if not low <= at_lane < high:
                continue
            at = start + at_lane - low
            taps = [up_tap(kx, *taps_of[shift]) for kx in range(3)]
            for x in range(4):
                value = zero_up
                for kx in range(3):
                    value = jnp.where(lane_f == 2 * x + kx - 1, taps[kx], value)
                up_out[at + 64 * x:at + 64 * x + 64] = value.astype(BF16)
    for number, shift in enumerate(((0, 0), (0, 1), (1, 0), (1, 1))):
        value = zero_up
        for k, (_, _, _, taps_of) in enumerate(CLASSES):
            if shift in taps_of:
                group = 4 * (k % 2) + (3 if k < 2 else 2)
                value = jnp.where(lane_f == group, up_tap(0, *taps_of[shift]), value)
        at = UP_MAIN + 64 * number
        up_out[at:at + 64] = value.astype(BF16)


def spread_octants(near_ref, octs, shifted, offset, start, stop):
    def shift_z(value, beyond):
        last = iota(value.shape, 0) % 4 == 3
        return jnp.where(last, pltpu.roll(beyond, 3, 0), pltpu.roll(value, 15, 0))

    def shift_y(value, beyond):
        first = iota(value.shape, 0) < 4
        return pltpu.roll(jnp.where(first, beyond, value), 12, 0)

    low_lane16 = iota((16, 128), 1) < 64

    def spread_octant(h):
        at = [near_ref[column, h] for column in upward_columns]
        here, z_next, y_next, yz_next = octs[h + offset], octs[at[0]], octs[at[1]], octs[at[2]]
        by_z = shift_z(here, z_next)
        x0, xz, xy, xyz = [octs[at[j], :, 0:128] for j in (3, 4, 5, 6)]
        x_by_z = shift_z(x0, xz)
        x_by_y = shift_y(x0, xy)
        x_by_yz = shift_y(x_by_z, shift_z(xy, xyz))
        return [
            (0, shift_y(here, y_next)),
            (256, here),
            (512, by_z),
            (768, shift_y(by_z, shift_z(y_next, yz_next))),
            (1024, jnp.where(low_lane16, x0, pltpu.roll(x_by_z, 64, 1))),
            (1152, jnp.where(low_lane16, x_by_y, pltpu.roll(x_by_yz, 64, 1))),
        ]

    def group_of(group, _):
        for h, parts in [(group * SPREAD + k, spread_octant(group * SPREAD + k)) for k in range(SPREAD)]:
            for lane, value in parts:
                shifted[h, :, lane:lane + value.shape[1]] = value.astype(BF16)
        return 0

    lax.fori_loop(start // SPREAD, stop // SPREAD, group_of, 0)


def upsample(shifted, up_w, up_bias, hidden, start, count, offset=0):
    def product(low, high, at):
        rows = shifted[pl.ds(start, count), :, low:high].reshape(16 * count, high - low)
        return jnp.dot(rows, up_w[at:at + high - low], preferred_element_type=F32)

    halo = product(HALO_AT, HALO_AT + 256, UP_MAIN)
    reached = iota((16 * count, 128), 1) >= 96
    for k, (((py, pz), low, high, _), at) in enumerate(zip(CLASSES, class_starts)):
        beyond = halo[:, 128 * (k % 2):128 * (k % 2) + 128]
        if k >= 2:
            beyond = pltpu.roll(beyond, 32, 1)
        value = product(low, high, at) + up_bias
        tiles = [value[:, 0:128], value[:, 128:256] + jnp.where(reached, beyond, 0.0)]
        for tile in range(2):
            half = 0.5 * tiles[tile]
            value = half + half * jnp.tanh(half)
            for b in range(count):
                for y in range(4):
                    hidden[tile, start + b + offset, pl.ds(8 * (2 * y + py) + pz, 4, stride=2), :] = (
                        value[16 * b + 4 * y:16 * b + 4 * y + 4])


def convolver(nearby, offset, hidden, conv_w, conv_bias, out_ref, out_offset):
    row = iota((8, 128), 0)
    first_row, last_row = row == 0, row == 7
    low_lane8 = iota((8, 128), 1) < 64
    lane = iota((8, 128), 1)
    even_lane = (lane < 32) | (lane >= 96)
    low_lane32 = iota((32, 128), 1) < 64

    def shift_row(dz, value, beyond):
        if dz == 0:
            return value
        if dz == 1:
            return pltpu.roll(jnp.where(first_row, beyond, value), 7, 0)
        return pltpu.roll(jnp.where(last_row, beyond, value), 1, 0)

    def two(one, other):
        return jnp.concatenate([one, other], axis=0).astype(BF16)

    def build(patches, b, k):
        at = {delta: nearby(column, b) for delta, column in column_of.items()}
        at[(0, 0, 0)] = b + offset

        def sheet(delta, y, tile):
            return hidden[tile, at[delta], 8 * y:8 * y + 8, :]

        def side(dy, dz, y):
            return jnp.where(low_lane8, sheet((1, dy, dz), y, 0), sheet((-1, dy, dz), y, 1))

        def sheets(dz, take):
            listed = []
            for step in range(10):
                dy = -1 if step == 0 else (1 if step == 9 else 0)
                y = (step - 1) % 8
                beyond = None if dz == 0 else take(dy, dz, y)
                listed.append(shift_row(dz, take(dy, 0, y), beyond))
            return listed

        def put(values, ky, at_lane):
            for pair in range(4):
                patches[k, 16 * pair:16 * pair + 16, at_lane:at_lane + 128] = values[pair]

        def put_all(listed, lanes):
            even = [two(listed[2 * n], listed[2 * n + 1]) for n in range(5)]
            odd = [two(listed[2 * n + 1], listed[2 * n + 2]) for n in range(4)]
            put(even[0:4], 0, lanes[0])
            put(odd, 1, lanes[1])
            put(even[1:5], 2, lanes[2])

        for dz in (-1, 0, 1):
            for tile in range(2):
                listed = sheets(dz, lambda dy, dz_, y: sheet((0, dy, dz_), y, tile))
                put_all(listed, [256 * (3 * ky + dz + 1) + 128 * tile for ky in range(3)])
        sides = [sheets(dz, side) for dz in (-1, 0, 1)]
        joined = [jnp.where(even_lane, one, pltpu.roll(other, 64, 1)) for one, other in zip(sides[0], sides[1])]
        put_all(joined, [EXTRA_AT + 128 * ky for ky in range(3)])
        last = sides[2]
        paired = [jnp.where(even_lane, last[n], pltpu.roll(last[n + 1], 64, 1)) for n in range(8)]
        put([two(paired[2 * n], paired[2 * n + 1]) for n in range(4)], 0, EXTRA_AT + 384)
        put([two(last[2 * n + 2], last[2 * n + 3]) for n in range(4)], 0, EXTRA_AT + 512)

    def convolve(patches, base):
        value = jnp.dot(patches[...].reshape(64 * GROUP, CONV_K), conv_w[...], preferred_element_type=F32) + conv_bias
        for pair in range(GROUP // 2):
            for half in range(2):
                turned = value[128 * pair:128 * pair + 128, 128 * half:128 * half + 128].T
                for x in range(0, 4, 2):
                    one, other = turned[32 * x:32 * x + 32], turned[32 * x + 32:32 * x + 64]
                    at = 256 * half + 64 * x
                    b = base + 2 * pair
                    out_ref[b - out_offset, :, at:at + 128] = jnp.where(
                        low_lane32, one, pltpu.roll(other, 64, 1)).astype(BF16)
                    out_ref[b + 1 - out_offset, :, at:at + 128] = jnp.where(
                        low_lane32, pltpu.roll(one, 64, 1), other).astype(BF16)

    def build_group(patches, base):
        for k in range(GROUP):
            build(patches, base + k, k)

    return build_group, convolve


def main_kernel(near_ref, octs, up_w, conv_w, bias, inner_hidden, inner_out, out_hbm,
                shifted, hidden, patches_0, patches_1, out_ref, out_sem, inner_sem):
    known = pl.ds(HALO, 2 * HALO)
    bring = pltpu.make_async_copy(inner_hidden.at[:, known], hidden.at[:, known], inner_sem.at[0])
    bring.start()
    done = pltpu.make_async_copy(inner_out, out_hbm.at[HALO:OWN], inner_sem.at[1])
    done.start()
    hidden[:, SLOTS] = jnp.zeros((2, 64, 128), F32)
    spread_octants(near_ref, octs, shifted, 0, 0, HALO)
    upsample(shifted, up_w, bias[0:1], hidden, 0, HALO)
    bring.wait()

    build_group, convolve = convolver(
        lambda column, b: near_ref[column, b + HALO], HALO, hidden, conv_w, bias[8:9], out_ref, 0)
    writes = []
    build_group(patches_0, 0)
    build_group(patches_1, GROUP)
    for number, patches in enumerate((patches_0, patches_1)):
        convolve(patches, number * GROUP)
        part = pl.ds(number * GROUP, GROUP)
        write = pltpu.make_async_copy(out_ref.at[part], out_hbm.at[part], out_sem.at[number])
        write.start()
        writes.append(write)
    for copy in [done] + writes:
        copy.wait()


VMEM = pl.BlockSpec(memory_space=pltpu.VMEM)
SMEM = pl.BlockSpec(memory_space=pltpu.SMEM)
ANY = pl.BlockSpec(memory_space=pltpu.MemorySpace.HBM)


def in_hbm(array):
    return pltpu.with_memory_space_constraint(array, pltpu.HBM)


def on_device(
    coarse_feat, coarse_children, fine_neighbours, up_weight, up_bias, conv_weight, conv_bias
):
    octs, near, up_w, conv_w, bias, inner_hidden, inner_out = pl.pallas_call(
        exchange_kernel,
        out_shape=[
            jax.ShapeDtypeStruct((SLOTS + 1, 16, 256), F32),
            jax.ShapeDtypeStruct((32, 128), jnp.int32),
            jax.ShapeDtypeStruct((UP_K, 256), BF16),
            jax.ShapeDtypeStruct((CONV_K, 256), BF16),
            jax.ShapeDtypeStruct((16, 256), F32),
            jax.ShapeDtypeStruct((2, ACTIVE + 1, 64, 128), F32),
            jax.ShapeDtypeStruct((INNER, 32, 512), BF16),
        ],
        in_specs=[ANY] * 7,
        out_specs=[VMEM] * 7,
        scratch_shapes=[
            pltpu.SMEM((8, 12), jnp.int32),
            pltpu.VMEM((26, OWN), jnp.int32),
            pltpu.VMEM((12, 64, 512), BF16),
            pltpu.VMEM((64, 864), BF16),
            pltpu.VMEM((1, 32), F32),
            pltpu.VMEM((32, 864), BF16),
            pltpu.VMEM((1, 32), F32),
            pltpu.VMEM((97, 16, 256), BF16),
            pltpu.VMEM((2 * OWN, 16, 256), BF16),
            pltpu.VMEM((8, 128), jnp.int32),
            pltpu.SMEM((8, 128), jnp.int32),
            pltpu.VMEM((OWN, 16, 256), BF16),
            pltpu.VMEM((OWN, 16, 256), BF16),
            pltpu.VMEM((2 * HALO, 16, 128), BF16),
            pltpu.VMEM((HALO, 16, 128), BF16),
            pltpu.VMEM((HALO, 16, 256), BF16),
            pltpu.VMEM((2 * HALO, 16, 128), BF16),
            pltpu.VMEM((HALO, 16, 128), BF16),
            pltpu.VMEM((HALO, 16, 256), BF16),
            pltpu.VMEM((32, 128), jnp.int32),
            pltpu.VMEM((32, 128), jnp.int32),
            pltpu.VMEM((32, 128), jnp.int32),
            pltpu.VMEM((64, 128), jnp.int32),
            pltpu.SMEM((64, 128), jnp.int32),
            pltpu.SMEM((32, 128), jnp.int32),
            pltpu.VMEM((ACTIVE, 16, 1280), BF16),
            pltpu.VMEM((GROUP, 64, CONV_K), BF16),
            pltpu.VMEM((GROUP, 64, CONV_K), BF16),
            pltpu.SemaphoreType.DMA((9,)),
            pltpu.SemaphoreType.DMA((9,)),
            pltpu.SemaphoreType.DMA((9,)),
            pltpu.SemaphoreType.DMA((12 // PACK,)),
        ],
        compiler_params=pltpu.CompilerParams(
            vmem_limit_bytes=32 * 2 ** 20, collective_id=0, has_side_effects=True),
        name="exchange",
    )(*[in_hbm(x) for x in (
        coarse_children.T, fine_neighbours.T, coarse_feat, up_weight, up_bias[None, :], conv_weight, conv_bias[None, :])])
    return pl.pallas_call(
        main_kernel,
        out_shape=jax.ShapeDtypeStruct((OWN, 32, 512), BF16),
        in_specs=[SMEM] + [VMEM] * 6,
        out_specs=ANY,
        scratch_shapes=[
            pltpu.VMEM((ACTIVE, 16, 1280), BF16),
            pltpu.VMEM((2, SLOTS + 1, 64, 128), F32),
            pltpu.VMEM((GROUP, 64, CONV_K), BF16),
            pltpu.VMEM((GROUP, 64, CONV_K), BF16),
            pltpu.VMEM((HALO, 32, 512), BF16),
            pltpu.SemaphoreType.DMA((2,)),
            pltpu.SemaphoreType.DMA((2,)),
        ],
        compiler_params=pltpu.CompilerParams(vmem_limit_bytes=28 * 2 ** 20),
        name="convolutions",
    )(near, octs, up_w, conv_w, bias, inner_hidden, inner_out)


def solution(mesh):
    in_specs = (
        P(AXES, None, None),
        P(AXES, None),
        P(AXES, None),
        P(),
        P(),
        P(),
        P(),
    )
    return jax.shard_map(
        on_device, mesh=mesh, in_specs=in_specs, out_specs=P(AXES, None, None), check_vma=False
    )
```

```python
import jax
import jax.numpy as jnp
from jax import lax
from jax.experimental import pallas as pl
from jax.experimental.pallas import tpu as pltpu
from jax.sharding import PartitionSpec as P

F32 = jnp.float32
BF16 = jnp.bfloat16
AXES = ("row", "col")
HALO = 12
OWN = 48
SLOTS = OWN + 3 * HALO
ACTIVE = OWN + 2 * HALO
REACH = 3 * OWN
PACK = 6
SPREAD = 6
GROUP = 6
INNER = OWN - HALO
EXTRA_AT = 9 * 256
CONV_K = EXTRA_AT + 5 * 128

direction_list = [
    (code // 9 - 1, code // 3 % 3 - 1, code % 3 - 1) for code in range(27) if code != 13
]
column_of = {delta: column for column, delta in enumerate(direction_list)}
upward_list = [(0, 0, 1), (0, 1, 0), (0, 1, 1), (1, 0, 0), (1, 0, 1), (1, 1, 0), (1, 1, 1)]
upward_columns = [column_of[delta] for delta in upward_list]

CLASSES = [
    ((0, 0), 256, 512, {(0, 0): (1, 1)}),
    ((0, 1), 256, 768, {(0, 0): (1, 2), (0, 1): (1, 0)}),
    ((1, 0), 0, 512, {(0, 0): (2, 1), (1, 0): (0, 1)}),
    ((1, 1), 0, 1024, {(0, 0): (2, 2), (0, 1): (2, 0), (1, 0): (0, 2), (1, 1): (0, 0)}),
]
SHIFT_AT = {(1, 0): 0, (0, 0): 256, (0, 1): 512, (1, 1): 768}
HALO_AT = 1024
class_starts = []
UP_MAIN = 0
for _, low, high, _ in CLASSES:
    class_starts.append(UP_MAIN)
    UP_MAIN += high - low
UP_K = UP_MAIN + 256


def iota(shape, dim):
    return lax.broadcasted_iota(jnp.int32, shape, dim)


def exchange_kernel(children_hbm, near_hbm, feat_hbm, up_hbm, up_b_hbm, conv_hbm, conv_b_hbm,
                    octs_ref, near_out, up_out, conv_out, bias_out, inner_hidden, inner_out,
                    children_ref, near_v, feat_ref, up_ref, up_b, conv_ref, conv_b,
                    table, slots, source_v, source, from_next, from_prev, low_own, edge_own, high_own, halo_next, edge_next, halo_prev,
                    near_pad, near_next, near_prev, inner_near_v, inner_near, all_near, shifted, patches_0, patches_1,
                    send_sem, recv_sem, fetch_sem, feat_sem):
    columns = lax.axis_size("col")
    ranks = lax.axis_size("row") * columns
    rank = lax.axis_index("row") * columns + lax.axis_index("col")
    exists = {-1: rank > 0, 1: rank < ranks - 1}

    def device(offset):
        other = lax.rem(rank + offset + ranks, ranks)
        return other // columns, lax.rem(other, columns)

    barrier = pltpu.get_barrier_semaphore()
    for offset in (1, -1):
        @pl.when(exists[offset])
        def _(offset=offset):
            pl.semaphore_signal(barrier, inc=1, device_id=device(offset), device_id_type=pl.DeviceIdType.MESH)

    fetches = [pltpu.make_async_copy(src, dst, fetch_sem.at[number]) for number, (src, dst) in enumerate((
        (children_hbm, children_ref), (near_hbm, near_v), (up_hbm, up_ref), (conv_hbm, conv_ref),
        (up_b_hbm, up_b), (conv_b_hbm, conv_b)))]

    def feat_fetch(step):
        part = pl.ds(step * PACK, PACK)
        return pltpu.make_async_copy(feat_hbm.at[part], feat_ref.at[part], feat_sem.at[step])

    fetches[0].start()
    for step in range(12 // PACK):
        feat_fetch(step).start()
    for fetch in fetches[1:]:
        fetch.start()

    fetches[0].wait()
    slot_id = iota((8, 128), 0) * 128 + iota((8, 128), 1)
    first = (rank - 1) * OWN
    chosen = jnp.full((8, 128), 96, jnp.int32)
    for c in range(12):
        for o in range(8):
            child = children_ref[o, c]
            position = jnp.where(child >= 0, child - first, REACH)
            chosen = jnp.where(slot_id == position, 8 * c + o, chosen)
    source_v[...] = chosen
    source_copy = pltpu.make_async_copy(source_v, source, fetch_sem.at[6])
    source_copy.start()

    low_lane = iota((64, 128), 1) < 64
    low_row = iota((8, 128), 0) < 4
    table[96] = jnp.zeros((16, 256), BF16)

    def turn(c, pair):
        near = feat_ref[c, :, 128 * pair:128 * pair + 128].astype(F32)
        far = feat_ref[c, :, 256 + 128 * pair:384 + 128 * pair].astype(F32)
        top = jnp.where(low_lane, near, pltpu.roll(far, 64, 1))
        bottom = jnp.where(low_lane, pltpu.roll(near, 64, 1), far)
        return jnp.concatenate([top, bottom], axis=0).T

    def octants_of(turned):
        listed = []
        for octant in range(8):
            ox, oy, oz = octant // 4, octant // 2 % 2, octant % 2
            sheets = []
            for y in range(4):
                at = 64 * ox + 8 * (4 * oy + y)
                sheets.append(turned[at:at + 8])
            halves = []
            for one, two in ((sheets[0], sheets[1]), (sheets[2], sheets[3])):
                if oz == 0:
                    halves.append(jnp.where(low_row, one, pltpu.roll(two, 4, 0)))
                else:
                    halves.append(jnp.where(low_row, pltpu.roll(one, 4, 0), two))
            listed.append(jnp.concatenate(halves, axis=0).astype(BF16))
        return listed

    def coarse_blocks(step, _):
        feat_fetch(step).wait()
        turned = [[turn(step * PACK + k, pair) for pair in range(2)] for k in range(PACK)]
        for k in range(PACK):
            for pair in range(2):
                for octant, value in enumerate(octants_of(turned[k][pair])):
                    table[(step * PACK + k) * 8 + octant, :, 128 * pair:128 * pair + 128] = value
        return 0

    lax.fori_loop(0, 12 // PACK, coarse_blocks, 0)
    source_copy.wait()
    fetches[1].wait()
    near_pad[...] = jnp.zeros((32, 128), jnp.int32)
    near_pad[0:26, 0:48] = near_v[...]
    inside = near_pad[...] - rank * OWN
    within = (near_pad[...] >= 0) & (inside >= 0) & (inside < OWN + HALO)
    inner_near_v[0:32] = jnp.where(within, inside + HALO, SLOTS)
    inner_near_v[32:64] = jnp.where(within, inside + HALO, ACTIVE)
    inner_copy = pltpu.make_async_copy(inner_near_v, inner_near, fetch_sem.at[7])
    inner_copy.start()

    def octant_at(q):
        return table[source[q // 128, q % 128]]

    def fill(start, q_start):
        def body(k, _):
            for j in range(8):
                slots[start + k * 8 + j] = octant_at(q_start + k * 8 + j)
            return 0
        lax.fori_loop(0, OWN // 16, body, 0)

    half = OWN // 2
    plan = [
        (slots.at[0:half], from_next.at[0:half], -1),
        (slots.at[OWN:OWN + half], from_prev.at[0:half], 1),
        (slots.at[half:OWN], from_next.at[half:OWN], -1),
        (slots.at[OWN + half:2 * OWN], from_prev.at[half:OWN], 1),
        (near_pad, near_next, -1),
        (near_pad, near_prev, 1),
        (low_own, halo_next, -1),
        (high_own, halo_prev, 1),
        (edge_own, edge_next, -1),
    ]

    def transfer(number):
        src, dst, offset = plan[number]
        return pltpu.make_async_remote_copy(
            src_ref=src, dst_ref=dst, send_sem=send_sem.at[number], recv_sem=recv_sem.at[number],
            device_id=device(offset), device_id_type=pl.DeviceIdType.MESH)

    def send(*numbers):
        for number in numbers:
            @pl.when(exists[plan[number][2]])
            def _(number=number):
                transfer(number).start()

    def sent(*numbers):
        for number in numbers:
            @pl.when(exists[plan[number][2]])
            def _(number=number):
                transfer(number).wait_send()

    def landed(*numbers):
        for number in numbers:
            @pl.when(exists[-plan[number][2]])
            def _(number=number):
                transfer(number).wait_recv()

    for offset, refs, near in ((1, (from_next, halo_next, edge_next), near_next), (-1, (from_prev, halo_prev), near_prev)):
        @pl.when(jnp.logical_not(exists[offset]))
        def _(refs=refs, near=near):
            for ref in refs:
                ref[...] = jnp.zeros(ref.shape, BF16)
            near[...] = jnp.full((32, 128), -1, jnp.int32)

    fill(0, 0)
    fill(OWN, 2 * OWN)
    pl.semaphore_wait(barrier, exists[1].astype(jnp.int32) + exists[-1].astype(jnp.int32))
    send(0, 1)
    fill(half, half)
    fill(OWN + half, 2 * OWN + half)
    send(2, 3, 4, 5)

    for fetch in fetches[2:]:
        fetch.wait()
    make_weights(up_ref, conv_ref, up_out, conv_out)
    spread = (iota((32, 256), 0) == iota((32, 256), 1) % 32).astype(F32)
    for number, ref in enumerate((up_b, conv_b)):
        bias_out[8 * number:8 * number + 8] = jnp.dot(
            jnp.broadcast_to(ref[...], (8, 32)), spread, precision=lax.Precision.HIGHEST,
            preferred_element_type=F32)
    octs_ref[SLOTS] = jnp.zeros((16, 256), F32)
    inner_hidden[:, ACTIVE] = jnp.zeros((2, 64, 128), F32)
    inner_copy.wait()

    def join(start, stop, copy_ref, offset):
        def body(k, _):
            for j in range(4):
                b = start + k * 4 + j
                total = octant_at(OWN + b).astype(F32) + from_next[b].astype(F32) + from_prev[b].astype(F32)
                octs_ref[HALO + b] = total
                if copy_ref is not None:
                    copy_ref[b - offset] = total.astype(BF16)
            return 0
        lax.fori_loop(0, (stop - start) // 4, body, 0)

    sub = iota((8, 128), 0)

    def join_low(k, _):
        for j in range(2):
            edges = []
            for b in (k * 4 + 2 * j, k * 4 + 2 * j + 1):
                total = octant_at(OWN + b).astype(F32) + from_next[b].astype(F32) + from_prev[b].astype(F32)
                octs_ref[HALO + b] = total
                low_own[b] = total[:, 0:128].astype(BF16)
                first, second = total[0:8, 128:256], total[8:16, 128:256]
                edges.append(jnp.where(sub < 5, first, jnp.where(
                    sub == 5, pltpu.roll(second, 5, 0), pltpu.roll(second, 2, 0))))
            edge_own[k * 2 + j] = jnp.concatenate(edges, axis=0).astype(BF16)
        return 0

    landed(0, 1)
    lax.fori_loop(0, half // 4, join_low, 0)
    send(6, 8)

    up_bias = bias_out[0:1]
    spread_octants(inner_near, octs_ref, shifted, HALO, 0, HALO)
    upsample(shifted, up_out, up_bias, inner_hidden, 0, HALO, HALO)
    landed(2, 3)
    join(OWN - HALO, OWN, high_own, OWN - HALO)
    send(7)
    join(half, OWN - HALO, None, 0)

    landed(4, 5)
    lane = iota((32, 128), 1)
    near = jnp.where(lane < HALO, pltpu.roll(near_prev[...], 128 - (OWN - HALO), 1),
                     jnp.where(lane < HALO + OWN, pltpu.roll(near_pad[...], HALO, 1),
                               pltpu.roll(near_next[...], HALO + OWN, 1)))
    moved = near - (rank * OWN - HALO)
    near_out[...] = jnp.where((near >= 0) & (moved >= 0) & (moved < SLOTS), moved, SLOTS)
    near_copy = pltpu.make_async_copy(near_out, all_near, fetch_sem.at[8])
    near_copy.start()

    spread_octants(inner_near, octs_ref, shifted, HALO, HALO, INNER)
    upsample(shifted, up_out, up_bias, inner_hidden, HALO, INNER - HALO, HALO)
    build_group, convolve = convolver(
        lambda column, b: inner_near[32 + column, b], HALO, inner_hidden, conv_out, bias_out[8:9], inner_out, HALO)

    def middle_groups(step, _):
        base = HALO + 2 * GROUP * step
        build_group(patches_0, base)
        build_group(patches_1, base + GROUP)
        convolve(patches_0, base)
        convolve(patches_1, base + GROUP)
        return 0

    lax.fori_loop(0, 1, middle_groups, 0)

    near_copy.wait()
    landed(6, 8)

    def spread_low(k, _):
        edges = edge_next[k].astype(F32)
        for j in range(2):
            u = HALO + OWN + 2 * k + j
            octs_ref[u, :, 0:128] = halo_next[2 * k + j].astype(F32)
            edge = edges[8 * j:8 * j + 8]
            octs_ref[u, 0:8, 128:256] = edge
            octs_ref[u, 8:16, 128:256] = jnp.where(sub == 0, pltpu.roll(edge, 3, 0), pltpu.roll(edge, 6, 0))
        return 0

    lax.fori_loop(0, HALO, spread_low, 0)
    spread_octants(all_near, octs_ref, shifted, 0, HALO + INNER, ACTIVE)
    upsample(shifted, up_out, up_bias, inner_hidden, HALO + INNER, 2 * HALO)
    lax.fori_loop(1, 3, middle_groups, 0)

    landed(7)
    octs_ref[0:HALO] = halo_prev[...].astype(F32)
    sent(*range(9))


def make_weights(up_ref, conv_ref, up_out, conv_out):
    spread = (iota((32, 256), 0) == iota((32, 256), 1) % 32).astype(BF16)
    lane_x = iota((32, 256), 1) // 32
    zero = jnp.zeros((32, 256), F32)
    wide = lax.dot_general(conv_ref[...], spread, (((0,), (0,)), ((), ())), preferred_element_type=F32)

    def tap_of(kx, ky, kz):
        at = 32 * (9 * kx + 3 * ky + kz)
        return wide[at:at + 32]

    for ky in range(3):
        for kz in range(3):
            taps = [tap_of(kx, ky, kz) for kx in range(3)]
            for x in range(8):
                value = zero
                for kx in range(3):
                    value = jnp.where(lane_x == x + 1 - kx, taps[kx], value)
                at = 256 * (3 * ky + kz) + 32 * x
                conv_out[at:at + 32] = value.astype(BF16)
    pairs = [((0, 0), (0, 1)), ((1, 0), (1, 1)), ((2, 0), (2, 1)), ((0, 2), (1, 2)), ((2, 2), None)]
    for tile, (even, odd) in enumerate(pairs):
        at = EXTRA_AT + 128 * tile

        def beyond(tap):
            return zero if tap is None else jnp.where(lane_x == 7, tap_of(2, *tap), zero)

        def before(tap):
            return zero if tap is None else jnp.where(lane_x == 0, tap_of(0, *tap), zero)

        conv_out[at:at + 32] = beyond(even).astype(BF16)
        conv_out[at + 32:at + 64] = before(odd).astype(BF16)
        conv_out[at + 64:at + 96] = beyond(odd).astype(BF16)
        conv_out[at + 96:at + 128] = before(even).astype(BF16)

    lane_f = iota((64, 256), 1) // 32
    zero_up = jnp.zeros((64, 256), F32)

    def up_tap(kx, ky, kz):
        code = 9 * kx + 3 * ky + kz
        return jnp.dot(up_ref[:, 32 * code:32 * code + 32], spread, preferred_element_type=F32)

    for (_, low, high, taps_of), start in zip(CLASSES, class_starts):
        for shift, at_lane in SHIFT_AT.items():
            if not low <= at_lane < high:
                continue
            at = start + at_lane - low
            taps = [up_tap(kx, *taps_of[shift]) for kx in range(3)]
            for x in range(4):
                value = zero_up
                for kx in range(3):
                    value = jnp.where(lane_f == 2 * x + kx - 1, taps[kx], value)
                up_out[at + 64 * x:at + 64 * x + 64] = value.astype(BF16)
    for number, shift in enumerate(((0, 0), (0, 1), (1, 0), (1, 1))):
        value = zero_up
        for k, (_, _, _, taps_of) in enumerate(CLASSES):
            if shift in taps_of:
                group = 4 * (k % 2) + (3 if k < 2 else 2)
                value = jnp.where(lane_f == group, up_tap(0, *taps_of[shift]), value)
        at = UP_MAIN + 64 * number
        up_out[at:at + 64] = value.astype(BF16)


def spread_octants(near_ref, octs, shifted, offset, start, stop):
    def shift_z(value, beyond):
        last = iota(value.shape, 0) % 4 == 3
        return jnp.where(last, pltpu.roll(beyond, 3, 0), pltpu.roll(value, 15, 0))

    def shift_y(value, beyond):
        first = iota(value.shape, 0) < 4
        return pltpu.roll(jnp.where(first, beyond, value), 12, 0)

    low_lane16 = iota((16, 128), 1) < 64

    def spread_octant(h):
        at = [near_ref[column, h] for column in upward_columns]
        here, z_next, y_next, yz_next = octs[h + offset], octs[at[0]], octs[at[1]], octs[at[2]]
        by_z = shift_z(here, z_next)
        x0, xz, xy, xyz = [octs[at[j], :, 0:128] for j in (3, 4, 5, 6)]
        x_by_z = shift_z(x0, xz)
        x_by_y = shift_y(x0, xy)
        x_by_yz = shift_y(x_by_z, shift_z(xy, xyz))
        return [
            (0, shift_y(here, y_next)),
            (256, here),
            (512, by_z),
            (768, shift_y(by_z, shift_z(y_next, yz_next))),
            (1024, jnp.where(low_lane16, x0, pltpu.roll(x_by_z, 64, 1))),
            (1152, jnp.where(low_lane16, x_by_y, pltpu.roll(x_by_yz, 64, 1))),
        ]

    def group_of(group, _):
        for h, parts in [(group * SPREAD + k, spread_octant(group * SPREAD + k)) for k in range(SPREAD)]:
            for lane, value in parts:
                shifted[h, :, lane:lane + value.shape[1]] = value.astype(BF16)
        return 0

    lax.fori_loop(start // SPREAD, stop // SPREAD, group_of, 0)


def upsample(shifted, up_w, up_bias, hidden, start, count, offset=0):
    def product(low, high, at):
        rows = shifted[pl.ds(start, count), :, low:high].reshape(16 * count, high - low)
        return jnp.dot(rows, up_w[at:at + high - low], preferred_element_type=F32)

    halo = product(HALO_AT, HALO_AT + 256, UP_MAIN)
    reached = iota((16 * count, 128), 1) >= 96
    for k, (((py, pz), low, high, _), at) in enumerate(zip(CLASSES, class_starts)):
        beyond = halo[:, 128 * (k % 2):128 * (k % 2) + 128]
        if k >= 2:
            beyond = pltpu.roll(beyond, 32, 1)
        value = product(low, high, at) + up_bias
        tiles = [value[:, 0:128], value[:, 128:256] + jnp.where(reached, beyond, 0.0)]
        for tile in range(2):
            half = 0.5 * tiles[tile]
            value = half + half * jnp.tanh(half)
            for b in range(count):
                for y in range(4):
                    hidden[tile, start + b + offset, pl.ds(8 * (2 * y + py) + pz, 4, stride=2), :] = (
                        value[16 * b + 4 * y:16 * b + 4 * y + 4])


def convolver(nearby, offset, hidden, conv_w, conv_bias, out_ref, out_offset):
    row = iota((8, 128), 0)
    first_row, last_row = row == 0, row == 7
    low_lane8 = iota((8, 128), 1) < 64
    lane = iota((8, 128), 1)
    even_lane = (lane < 32) | (lane >= 96)
    low_lane32 = iota((32, 128), 1) < 64

    def shift_row(dz, value, beyond):
        if dz == 0:
            return value
        if dz == 1:
            return pltpu.roll(jnp.where(first_row, beyond, value), 7, 0)
        return pltpu.roll(jnp.where(last_row, beyond, value), 1, 0)

    def two(one, other):
        return jnp.concatenate([one, other], axis=0).astype(BF16)

    def build(patches, b, k):
        at = {delta: nearby(column, b) for delta, column in column_of.items()}
        at[(0, 0, 0)] = b + offset

        def sheet(delta, y, tile):
            return hidden[tile, at[delta], 8 * y:8 * y + 8, :]

        def side(dy, dz, y):
            return jnp.where(low_lane8, sheet((1, dy, dz), y, 0), sheet((-1, dy, dz), y, 1))

        def sheets(dz, take):
            listed = []
            for step in range(10):
                dy = -1 if step == 0 else (1 if step == 9 else 0)
                y = (step - 1) % 8
                beyond = None if dz == 0 else take(dy, dz, y)
                listed.append(shift_row(dz, take(dy, 0, y), beyond))
            return listed

        def put(values, ky, at_lane):
            for pair in range(4):
                patches[k, 16 * pair:16 * pair + 16, at_lane:at_lane + 128] = values[pair]

        def put_all(listed, lanes):
            even = [two(listed[2 * n], listed[2 * n + 1]) for n in range(5)]
            odd = [two(listed[2 * n + 1], listed[2 * n + 2]) for n in range(4)]
            put(even[0:4], 0, lanes[0])
            put(odd, 1, lanes[1])
            put(even[1:5], 2, lanes[2])

        for dz in (-1, 0, 1):
            for tile in range(2):
                listed = sheets(dz, lambda dy, dz_, y: sheet((0, dy, dz_), y, tile))
                put_all(listed, [256 * (3 * ky + dz + 1) + 128 * tile for ky in range(3)])
        sides = [sheets(dz, side) for dz in (-1, 0, 1)]
        joined = [jnp.where(even_lane, one, pltpu.roll(other, 64, 1)) for one, other in zip(sides[0], sides[1])]
        put_all(joined, [EXTRA_AT + 128 * ky for ky in range(3)])
        last = sides[2]
        paired = [jnp.where(even_lane, last[n], pltpu.roll(last[n + 1], 64, 1)) for n in range(8)]
        put([two(paired[2 * n], paired[2 * n + 1]) for n in range(4)], 0, EXTRA_AT + 384)
        put([two(last[2 * n + 2], last[2 * n + 3]) for n in range(4)], 0, EXTRA_AT + 512)

    def convolve(patches, base):
        value = jnp.dot(patches[...].reshape(64 * GROUP, CONV_K), conv_w[...], preferred_element_type=F32) + conv_bias
        for pair in range(GROUP // 2):
            for half in range(2):
                turned = value[128 * pair:128 * pair + 128, 128 * half:128 * half + 128].T
                for x in range(0, 4, 2):
                    one, other = turned[32 * x:32 * x + 32], turned[32 * x + 32:32 * x + 64]
                    at = 256 * half + 64 * x
                    b = base + 2 * pair
                    out_ref[b - out_offset, :, at:at + 128] = jnp.where(
                        low_lane32, one, pltpu.roll(other, 64, 1)).astype(BF16)
                    out_ref[b + 1 - out_offset, :, at:at + 128] = jnp.where(
                        low_lane32, pltpu.roll(one, 64, 1), other).astype(BF16)

    def build_group(patches, base):
        for k in range(GROUP):
            build(patches, base + k, k)

    return build_group, convolve


def main_kernel(near_ref, octs, up_w, conv_w, bias, inner_hidden, inner_out, out_hbm,
                shifted, hidden, patches_0, patches_1, out_ref, out_sem, inner_sem):
    known = pl.ds(HALO, 2 * HALO)
    bring = pltpu.make_async_copy(inner_hidden.at[:, known], hidden.at[:, known], inner_sem.at[0])
    bring.start()
    done = pltpu.make_async_copy(inner_out, out_hbm.at[HALO:OWN], inner_sem.at[1])
    done.start()
    hidden[:, SLOTS] = jnp.zeros((2, 64, 128), F32)
    spread_octants(near_ref, octs, shifted, 0, 0, HALO)
    upsample(shifted, up_w, bias[0:1], hidden, 0, HALO)
    bring.wait()

    build_group, convolve = convolver(
        lambda column, b: near_ref[column, b + HALO], HALO, hidden, conv_w, bias[8:9], out_ref, 0)
    writes = []
    build_group(patches_0, 0)
    build_group(patches_1, GROUP)
    for number, patches in enumerate((patches_0, patches_1)):
        convolve(patches, number * GROUP)
        part = pl.ds(number * GROUP, GROUP)
        write = pltpu.make_async_copy(out_ref.at[part], out_hbm.at[part], out_sem.at[number])
        write.start()
        writes.append(write)
    for copy in [done] + writes:
        copy.wait()


VMEM = pl.BlockSpec(memory_space=pltpu.VMEM)
SMEM = pl.BlockSpec(memory_space=pltpu.SMEM)
ANY = pl.BlockSpec(memory_space=pltpu.MemorySpace.HBM)


def in_hbm(array):
    return pltpu.with_memory_space_constraint(array, pltpu.HBM)


def on_device(
    coarse_feat, coarse_children, fine_neighbours, up_weight, up_bias, conv_weight, conv_bias
):
    octs, near, up_w, conv_w, bias, inner_hidden, inner_out = pl.pallas_call(
        exchange_kernel,
        out_shape=[
            jax.ShapeDtypeStruct((SLOTS + 1, 16, 256), F32),
            jax.ShapeDtypeStruct((32, 128), jnp.int32),
            jax.ShapeDtypeStruct((UP_K, 256), BF16),
            jax.ShapeDtypeStruct((CONV_K, 256), BF16),
            jax.ShapeDtypeStruct((16, 256), F32),
            jax.ShapeDtypeStruct((2, ACTIVE + 1, 64, 128), F32),
            jax.ShapeDtypeStruct((INNER, 32, 512), BF16),
        ],
        in_specs=[ANY] * 7,
        out_specs=[VMEM] * 7,
        scratch_shapes=[
            pltpu.SMEM((8, 12), jnp.int32),
            pltpu.VMEM((26, OWN), jnp.int32),
            pltpu.VMEM((12, 64, 512), BF16),
            pltpu.VMEM((64, 864), BF16),
            pltpu.VMEM((1, 32), F32),
            pltpu.VMEM((32, 864), BF16),
            pltpu.VMEM((1, 32), F32),
            pltpu.VMEM((97, 16, 256), BF16),
            pltpu.VMEM((2 * OWN, 16, 256), BF16),
            pltpu.VMEM((8, 128), jnp.int32),
            pltpu.SMEM((8, 128), jnp.int32),
            pltpu.VMEM((OWN, 16, 256), BF16),
            pltpu.VMEM((OWN, 16, 256), BF16),
            pltpu.VMEM((2 * HALO, 16, 128), BF16),
            pltpu.VMEM((HALO, 16, 128), BF16),
            pltpu.VMEM((HALO, 16, 256), BF16),
            pltpu.VMEM((2 * HALO, 16, 128), BF16),
            pltpu.VMEM((HALO, 16, 128), BF16),
            pltpu.VMEM((HALO, 16, 256), BF16),
            pltpu.VMEM((32, 128), jnp.int32),
            pltpu.VMEM((32, 128), jnp.int32),
            pltpu.VMEM((32, 128), jnp.int32),
            pltpu.VMEM((64, 128), jnp.int32),
            pltpu.SMEM((64, 128), jnp.int32),
            pltpu.SMEM((32, 128), jnp.int32),
            pltpu.VMEM((ACTIVE, 16, 1280), BF16),
            pltpu.VMEM((GROUP, 64, CONV_K), BF16),
            pltpu.VMEM((GROUP, 64, CONV_K), BF16),
            pltpu.SemaphoreType.DMA((9,)),
            pltpu.SemaphoreType.DMA((9,)),
            pltpu.SemaphoreType.DMA((9,)),
            pltpu.SemaphoreType.DMA((12 // PACK,)),
        ],
        compiler_params=pltpu.CompilerParams(
            vmem_limit_bytes=32 * 2 ** 20, collective_id=0, has_side_effects=True),
        name="exchange",
    )(*[in_hbm(x) for x in (
        coarse_children.T, fine_neighbours.T, coarse_feat, up_weight, up_bias[None, :], conv_weight, conv_bias[None, :])])
    return pl.pallas_call(
        main_kernel,
        out_shape=jax.ShapeDtypeStruct((OWN, 32, 512), BF16),
        in_specs=[SMEM] + [VMEM] * 6,
        out_specs=ANY,
        scratch_shapes=[
            pltpu.VMEM((ACTIVE, 16, 1280), BF16),
            pltpu.VMEM((2, SLOTS + 1, 64, 128), F32),
            pltpu.VMEM((GROUP, 64, CONV_K), BF16),
            pltpu.VMEM((GROUP, 64, CONV_K), BF16),
            pltpu.VMEM((HALO, 32, 512), BF16),
            pltpu.SemaphoreType.DMA((2,)),
            pltpu.SemaphoreType.DMA((2,)),
        ],
        compiler_params=pltpu.CompilerParams(vmem_limit_bytes=28 * 2 ** 20),
        name="convolutions",
    )(near, octs, up_w, conv_w, bias, inner_hidden, inner_out)


def solution(mesh):
    in_specs = (
        P(AXES, None, None),
        P(AXES, None),
        P(AXES, None),
        P(),
        P(),
        P(),
        P(),
    )
    return jax.shard_map(
        on_device, mesh=mesh, in_specs=in_specs, out_specs=P(AXES, None, None), check_vma=False
    )
```
